256 devices in a mesh: dp: 2 (over x_hi), dap: 128 (over x_lo, z, y, core).
Axes of the slice: x: 4 (x_hi: 2, x_lo: 2; x = x_hi * 2 + x_lo), y: 4, z: 8, core: 2. Of those that a mesh axis runs over, the one named last changes fastest.
Arguments:
- pair: bfloat16 [2, 256, 256, 128], P('dp', 'dap'), may hold values from -6 to 6
- grad_out: bfloat16 [2, 256, 256, 128], P('dp', 'dap'), may hold values from -6 to 6
- w_in: bfloat16 [128, 512], replicated, may hold values from -0.5 to 0.5
- w_gate: bfloat16 [128, 128], replicated, may hold values from -0.5 to 0.5
- w_out: bfloat16 [128, 128], replicated, may hold values from -0.5 to 0.5
- ln_in_gain: float32 [128], replicated, may hold values from 0.1 to 1.9
- ln_in_bias: float32 [128], replicated, may hold values from -2 to 2
- ln_out_gain: float32 [128], replicated, may hold values from 0.1 to 1.9
- ln_out_bias: float32 [128], replicated, may hold values from -2 to 2
Outputs:
- pair_grad: bfloat16 [2, 256, 256, 128], P('dp', 'dap')
- w_in_grad: float32 [128, 512], replicated
- w_gate_grad: float32 [128, 128], replicated
- w_out_grad: float32 [128, 128], replicated
- ln_in_gain_grad: float32 [128], replicated
- ln_in_bias_grad: float32 [128], replicated
- ln_out_gain_grad: float32 [128], replicated
- ln_out_bias_grad: float32 [128], replicated
The draws below stay inside these ranges and needn't reach their ends.
All inputs are finite; a program needn't handle non-finite values.
Results may differ from the reference program's by a relative error of at most 0.008.
Values may be sent and summed in bfloat16 or wider, within the bound.
No kernel may reach another device: no remote copies, remote signals or barrier semaphores. Data moves between devices by JAX's collectives and lax.ppermute only.
A program may use at most 64 MiB of HBM per device.

```python
import math
import jax
import jax.numpy as jnp
from jax import lax

C = 128
H = 128
N = 256
B = 2


def steps_of(rng, shape, shards, smallest, largest):
    loudness = 1.0
    for position, shards_of in shards:
        heights = jax.random.uniform(jax.random.fold_in(jax.random.fold_in(rng, 6), position), (shards_of,), jnp.float32, smallest / len(shards), largest / len(shards))
        loudness = loudness * jnp.repeat(jnp.exp(heights), shape[position] // shards_of).reshape((-1,) + (1,) * (len(shape) - 1 - position))
    return loudness


def bell_draw(stream_key, extent, spread, bound, cuts=(), held_as=jnp.bfloat16):
    level = steps_of(stream_key, extent, cuts, -0.22, 0.18) if cuts else 1.0
    values = jax.random.normal(stream_key, extent, jnp.float32) * spread * level
    return jnp.minimum(jnp.maximum(values, -bound), bound).astype(held_as)


def setup_inputs(seed: int = 0) -> dict:
    seeds = jax.random.split(jax.random.key(seed), 10)
    return {
        "pair": bell_draw(seeds[0], (B, N, N, C), 1.0, 6.0, ((0, 2), (1, 128))),
        "grad_out": bell_draw(seeds[1], (B, N, N, C), 1.0, 6.0, ((0, 2), (1, 128))),
        "w_in": bell_draw(seeds[2], (C, 4 * H), C ** -0.5, 0.5),
        "w_gate": bell_draw(seeds[3], (C, C), C ** -0.5, 0.5),
        "w_out": bell_draw(seeds[4], (H, C), H ** -0.5, 0.5),
        "ln_in_gain": jnp.clip(1.0 + 0.18 * jax.random.normal(seeds[5], (C,), jnp.float32), 0.1, 1.9),
        "ln_in_bias": bell_draw(seeds[6], (C,), 0.5, 2.0, (), jnp.float32),
        "ln_out_gain": jnp.clip(1.0 + 0.18 * jax.random.normal(seeds[7], (H,), jnp.float32), 0.1, 1.9),
        "ln_out_bias": bell_draw(seeds[8], (H,), 0.5, 2.0, (), jnp.float32),
    }


EPSILON = 1e-05

def normalize(values, gain, bias):
    center = values - lax.optimization_barrier(jnp.mean(values, axis=-1, keepdims=True))
    scale_inv = lax.rsqrt(lax.optimization_barrier(jnp.mean(center * center, axis=-1, keepdims=True)) + EPSILON)
    normed_hat = center * scale_inv
    return (normed_hat * gain + bias, normed_hat, scale_inv)

def norm_back(grad_normed, normed_hat, scale_inv, gain):
    scaled = grad_normed * gain
    return scale_inv * (scaled - lax.optimization_barrier(jnp.mean(scaled, axis=-1, keepdims=True)) - normed_hat * lax.optimization_barrier(jnp.mean(scaled * normed_hat, axis=-1, keepdims=True)))

def gated_terms(normed_rows, w_in):
    hidden = w_in.shape[1] // 4
    projected = jnp.dot(normed_rows, w_in, preferred_element_type=jnp.float32)
    return (projected[..., :hidden], projected[..., hidden:2 * hidden], projected[..., 2 * hidden:3 * hidden], projected[..., 3 * hidden:])

def reference(pair, grad_out, w_in, w_gate, w_out, ln_in_gain, ln_in_bias, ln_out_gain, ln_out_bias):
    count = pair.shape[0]
    full_len = pair.shape[1]
    channels = pair.shape[3]
    hidden = w_out.shape[0]
    block = math.gcd(full_len, 64)
    nblocks = full_len // block
    chan_block = math.gcd(hidden, 8)
    w_in_total = jnp.zeros((channels, 4 * hidden), jnp.float32)
    w_gate_total = jnp.zeros((channels, channels), jnp.float32)
    w_out_total = jnp.zeros((hidden, channels), jnp.float32)
    in_gain_total = jnp.zeros((channels,), jnp.float32)
    in_bias_total = jnp.zeros((channels,), jnp.float32)
    out_gain_total = jnp.zeros((hidden,), jnp.float32)
    out_bias_total = jnp.zeros((hidden,), jnp.float32)
    pair_grads = []

    def front(pair_rows):
        normed_f, unused_hat, unused_scale = normalize(pair_rows.astype(jnp.float32), ln_in_gain, ln_in_bias)
        normed_rows = normed_f.astype(jnp.bfloat16)
        proj_left, gate_left, proj_right, gate_right = gated_terms(normed_rows, w_in)
        left_rows = (jax.nn.sigmoid(gate_left) * proj_left).astype(jnp.bfloat16)
        right_rows = (jax.nn.sigmoid(gate_right) * proj_right).astype(jnp.bfloat16)
        return (normed_rows, left_rows, right_rows)

    def contract(operands):
        lefts, rights = operands
        return jnp.einsum('hik,hjk->hij', lefts.astype(jnp.float32), rights.astype(jnp.float32)).astype(jnp.bfloat16)

    def middle(operands):
        normed_rows, product_rows, grad_rows = operands
        out_f, out_hat, out_scale = normalize(product_rows.astype(jnp.float32), ln_out_gain, ln_out_bias)
        out_normed = out_f.astype(jnp.bfloat16)
        outlin = jnp.dot(out_normed, w_out, preferred_element_type=jnp.float32)
        gate = jax.nn.sigmoid(jnp.dot(normed_rows, w_gate, preferred_element_type=jnp.float32))
        grad32 = grad_rows.astype(jnp.float32)
        grad_lin = (grad32 * gate).astype(jnp.bfloat16)
        grad_gate = (grad32 * outlin * gate * (1.0 - gate)).astype(jnp.bfloat16)
        w_out_part = jnp.dot(out_normed.reshape(-1, hidden).T, grad_lin.reshape(-1, channels), preferred_element_type=jnp.float32)
        w_gate_part = jnp.dot(normed_rows.reshape(-1, channels).T, grad_gate.reshape(-1, channels), preferred_element_type=jnp.float32)
        grad_out_normed = jnp.dot(grad_lin, w_out.T, preferred_element_type=jnp.float32)
        grad_product = norm_back(grad_out_normed, out_hat, out_scale, ln_out_gain).astype(jnp.bfloat16)
        gain_part = lax.optimization_barrier(jnp.sum(grad_out_normed * out_hat, axis=(0, 1)))
        bias_part = lax.optimization_barrier(jnp.sum(grad_out_normed, axis=(0, 1)))
        return (grad_product, grad_gate, w_out_part, w_gate_part, gain_part, bias_part)

    def contract_back(operands):
        grads, lefts, rights = operands
        grads32 = grads.astype(jnp.float32)
        grad_left = jnp.einsum('hij,hjk->hik', grads32, rights.astype(jnp.float32)).astype(jnp.bfloat16)
        grad_right = jnp.einsum('hij,hik->hjk', grads32, lefts.astype(jnp.float32)).astype(jnp.bfloat16)
        return (grad_left, grad_right)

    def rear(operands):
        pair_rows, normed_rows, grad_left, grad_right, grad_gate = operands
        unused_normed, pair_hat, pair_scale = normalize(pair_rows.astype(jnp.float32), ln_in_gain, ln_in_bias)
        proj_left, gate_left, proj_right, gate_right = gated_terms(normed_rows, w_in)
        sig_left = jax.nn.sigmoid(gate_left)
        sig_right = jax.nn.sigmoid(gate_right)
        left32 = grad_left.astype(jnp.float32)
        right32 = grad_right.astype(jnp.float32)
        grad_projected = jnp.concatenate([left32 * sig_left, left32 * proj_left * sig_left * (1.0 - sig_left), right32 * sig_right, right32 * proj_right * sig_right * (1.0 - sig_right)], axis=-1).astype(jnp.bfloat16)
        w_in_part = jnp.dot(normed_rows.reshape(-1, channels).T, grad_projected.reshape(-1, 4 * hidden), preferred_element_type=jnp.float32)
        grad_normed = jnp.dot(grad_projected, w_in.T, preferred_element_type=jnp.float32) + jnp.dot(grad_gate, w_gate.T, preferred_element_type=jnp.float32)
        grad_pair = norm_back(grad_normed, pair_hat, pair_scale, ln_in_gain).astype(jnp.bfloat16)
        return (grad_pair, w_in_part, lax.optimization_barrier(jnp.sum(grad_normed * pair_hat, axis=(0, 1))), lax.optimization_barrier(jnp.sum(grad_normed, axis=(0, 1))))
    for member in range(count):
        pair_blocks = pair[member].reshape(nblocks, block, full_len, channels)
        grad_blocks = grad_out[member].reshape(nblocks, block, full_len, channels)
        normed_blocks, left_blocks, right_blocks = lax.map(front, pair_blocks)
        left_t = jnp.transpose(left_blocks.reshape(full_len, full_len, hidden), (2, 0, 1))
        right_t = jnp.transpose(right_blocks.reshape(full_len, full_len, hidden), (2, 0, 1))
        left_c = left_t.reshape(hidden // chan_block, chan_block, full_len, full_len)
        right_c = right_t.reshape(hidden // chan_block, chan_block, full_len, full_len)
        product_t = lax.map(contract, (left_c, right_c)).reshape(hidden, full_len, full_len)
        product = jnp.transpose(product_t, (1, 2, 0)).reshape(nblocks, block, full_len, hidden)
        grad_product, grad_gate, w_out_parts, w_gate_parts, gain_parts, bias_parts = lax.map(middle, (normed_blocks, product, grad_blocks))
        w_out_total = w_out_total + lax.optimization_barrier(jnp.sum(w_out_parts, axis=0))
        w_gate_total = w_gate_total + lax.optimization_barrier(jnp.sum(w_gate_parts, axis=0))
        out_gain_total = out_gain_total + lax.optimization_barrier(jnp.sum(gain_parts, axis=0))
        out_bias_total = out_bias_total + lax.optimization_barrier(jnp.sum(bias_parts, axis=0))
        grad_t = jnp.transpose(grad_product.reshape(full_len, full_len, hidden), (2, 0, 1))
        grad_c = grad_t.reshape(hidden // chan_block, chan_block, full_len, full_len)
        grad_left_c, grad_right_c = lax.map(contract_back, (grad_c, left_c, right_c))
        grad_left = jnp.transpose(grad_left_c.reshape(hidden, full_len, full_len), (1, 2, 0))
        grad_right = jnp.transpose(grad_right_c.reshape(hidden, full_len, full_len), (1, 2, 0))
        grad_pair, w_in_parts, in_gain_parts, in_bias_parts = lax.map(rear, (pair_blocks, normed_blocks, grad_left.reshape(nblocks, block, full_len, hidden), grad_right.reshape(nblocks, block, full_len, hidden), grad_gate))
        w_in_total = w_in_total + lax.optimization_barrier(jnp.sum(w_in_parts, axis=0))
        in_gain_total = in_gain_total + lax.optimization_barrier(jnp.sum(in_gain_parts, axis=0))
        in_bias_total = in_bias_total + lax.optimization_barrier(jnp.sum(in_bias_parts, axis=0))
        pair_grads.append(grad_pair.reshape(full_len, full_len, channels))
    return (jnp.stack(pair_grads), w_in_total, w_gate_total, w_out_total, in_gain_total, in_bias_total, out_gain_total, out_bias_total)
```

```python
import jax
import jax.numpy as jnp
from jax import lax
from jax.sharding import Mesh, PartitionSpec as P

EPSILON = 1e-05
DAP = ("x", "z", "y", "c")
PEERS = ("X", "x", "z", "y")


def normalize(values, gain, bias, axis):
    center = values - jnp.mean(values, axis=axis, keepdims=True)
    scale_inv = lax.rsqrt(jnp.mean(center * center, axis=axis, keepdims=True) + EPSILON)
    normed_hat = center * scale_inv
    return (normed_hat * gain + bias, normed_hat, scale_inv)


def norm_back(grad_normed, normed_hat, scale_inv, gain, axis):
    scaled = grad_normed * gain
    return scale_inv * (
        scaled
        - jnp.mean(scaled, axis=axis, keepdims=True)
        - normed_hat * jnp.mean(scaled * normed_hat, axis=axis, keepdims=True)
    )


def edge_terms(normed_rows, weights, hidden):
    projected = jnp.einsum(
        "brkc,cf->bfrk", normed_rows, weights, preferred_element_type=jnp.float32
    )
    return (projected[:, :hidden], projected[:, hidden:])


def total_over_devices(matrices, vectors):
    core = lax.axis_index("c")
    swap = [(0, 1), (1, 0)]
    rows, width = matrices.shape
    half = rows // 2
    peers = lax.axis_size(PEERS)
    parts = matrices.reshape(2, peers, half * width // peers // 128, 128)
    vec = vectors.reshape(2, peers, 1, vectors.size // 2 // peers)
    vec = jnp.pad(vec, ((0, 0), (0, 0), (0, 0), (0, 128 - vec.shape[-1])))
    parts = jnp.concatenate([parts, vec], axis=2)
    keep = jnp.where(core == 0, parts[0], parts[1])
    give = jnp.where(core == 0, parts[1], parts[0])
    keep = keep + lax.ppermute(give, "c", swap)
    share = lax.all_to_all(keep, PEERS, 0, 0, tiled=True)
    share = jnp.sum(share, axis=0, keepdims=True)
    mine = lax.all_to_all(
        jnp.broadcast_to(share, keep.shape), PEERS, 0, 0, tiled=True
    )
    other = lax.ppermute(mine, "c", swap)
    low = jnp.where(core == 0, mine, other)
    high = jnp.where(core == 0, other, mine)
    both = jnp.stack([low, high])
    total = both[:, :, :-1].reshape(rows, width)
    vec_total = both[:, :, -1, : vectors.size // 2 // peers].reshape(vectors.shape)
    return total, vec_total


def on_device(
    pair, grad_out, w_in, w_gate, w_out, ln_in_gain, ln_in_bias, ln_out_gain, ln_out_bias
):
    batch, row_count, full_len, channels = pair.shape
    hidden = w_out.shape[0]
    groups = lax.axis_size(DAP)
    share = hidden // groups
    pair_f, pair_hat, pair_scale = normalize(pair.astype(jnp.float32), ln_in_gain, ln_in_bias, 3)
    pair_normed = pair_f.astype(jnp.bfloat16)
    proj_left, gate_left = edge_terms(pair_normed, w_in[:, : 2 * hidden], hidden)
    proj_right, gate_right = edge_terms(pair_normed, w_in[:, 2 * hidden :], hidden)
    sig_left = jax.nn.sigmoid(gate_left)
    sig_right = jax.nn.sigmoid(gate_right)
    left_split = (
        (sig_left * proj_left)
        .astype(jnp.bfloat16)
        .reshape(batch, groups, share, row_count, full_len)
    )
    right_split = (
        (sig_right * proj_right)
        .astype(jnp.bfloat16)
        .reshape(batch, groups, share, row_count, full_len)
    )
    edges = jnp.stack([left_split[0, :, 0], right_split[0, :, 0]], axis=1)
    edge_cols = lax.all_to_all(edges, DAP, 0, 0, tiled=True)
    left_cols = edge_cols[:, 0].reshape(full_len, full_len)
    right_cols = edge_cols[:, 1].reshape(full_len, full_len)
    product_cols = jnp.einsum(
        "ik,jk->ij", left_cols, right_cols, preferred_element_type=jnp.float32
    ).astype(jnp.bfloat16)
    product_t = lax.all_to_all(
        product_cols.reshape(groups, row_count, full_len), DAP, 0, 0, tiled=True
    ).reshape(batch, hidden, row_count, full_len)
    out_gain_b = ln_out_gain.reshape(1, hidden, 1, 1)
    out_f, out_hat, out_scale = normalize(
        product_t.astype(jnp.float32), out_gain_b, ln_out_bias.reshape(1, hidden, 1, 1), 1
    )
    out_normed = out_f.astype(jnp.bfloat16)
    outlin = jnp.einsum("bhrk,hc->brkc", out_normed, w_out, preferred_element_type=jnp.float32)
    gate = jax.nn.sigmoid(
        jnp.einsum("brkc,cd->brkd", pair_normed, w_gate, preferred_element_type=jnp.float32)
    )
    grad32 = grad_out.astype(jnp.float32)
    grad_lin = (grad32 * gate).astype(jnp.bfloat16)
    grad_gate = (grad32 * outlin * gate * (1.0 - gate)).astype(jnp.bfloat16)
    w_out_part = jnp.einsum(
        "bhrk,brkc->hc", out_normed, grad_lin, preferred_element_type=jnp.float32
    )
    w_gate_part = jnp.einsum(
        "brkc,brkd->cd", pair_normed, grad_gate, preferred_element_type=jnp.float32
    )
    grad_out_normed = jnp.einsum(
        "brkc,hc->bhrk", grad_lin, w_out, preferred_element_type=jnp.float32
    )
    grad_product = norm_back(grad_out_normed, out_hat, out_scale, out_gain_b, 1).astype(
        jnp.bfloat16
    )
    out_gain_part = jnp.sum(grad_out_normed * out_hat, axis=(0, 2, 3))
    out_bias_part = jnp.sum(grad_out_normed, axis=(0, 2, 3))
    grad_cols = lax.all_to_all(
        grad_product.reshape(groups, row_count, full_len), DAP, 0, 0, tiled=True
    ).reshape(full_len, full_len)
    grad_left_cols = jnp.einsum(
        "ij,jk->ik", grad_cols, right_cols, preferred_element_type=jnp.float32
    ).astype(jnp.bfloat16)
    grad_right_cols = jnp.einsum(
        "ij,ik->jk", grad_cols, left_cols, preferred_element_type=jnp.float32
    ).astype(jnp.bfloat16)
    grad_edge_cols = jnp.stack(
        [
            grad_left_cols.reshape(groups, row_count, full_len),
            grad_right_cols.reshape(groups, row_count, full_len),
        ],
        axis=1,
    )
    grad_edges = lax.all_to_all(grad_edge_cols, DAP, 0, 0, tiled=True)
    grad_left_t = grad_edges[:, 0]
    grad_right_t = grad_edges[:, 1]
    left32 = grad_left_t.reshape(batch, hidden, row_count, full_len).astype(jnp.float32)
    right32 = grad_right_t.reshape(batch, hidden, row_count, full_len).astype(jnp.float32)
    grad_projected = jnp.concatenate(
        [
            left32 * sig_left,
            left32 * proj_left * sig_left * (1.0 - sig_left),
            right32 * sig_right,
            right32 * proj_right * sig_right * (1.0 - sig_right),
        ],
        axis=1,
    ).astype(jnp.bfloat16)
    w_in_part = jnp.einsum(
        "brkc,bfrk->cf", pair_normed, grad_projected, preferred_element_type=jnp.float32
    )
    grad_normed = jnp.einsum(
        "bfrk,cf->brkc", grad_projected, w_in, preferred_element_type=jnp.float32
    ) + jnp.einsum("brkd,cd->brkc", grad_gate, w_gate, preferred_element_type=jnp.float32)
    pair_grad = norm_back(grad_normed, pair_hat, pair_scale, ln_in_gain, 3).astype(jnp.bfloat16)
    in_gain_part = jnp.sum(grad_normed * pair_hat, axis=(0, 1, 2))
    in_bias_part = jnp.sum(grad_normed, axis=(0, 1, 2))
    matrices, vectors = total_over_devices(
        jnp.concatenate([w_in_part, w_gate_part, w_out_part], axis=1),
        jnp.stack([in_gain_part, in_bias_part, out_gain_part, out_bias_part]),
    )
    w_in_total = matrices[:, : 4 * hidden]
    w_gate_total = matrices[:, 4 * hidden : 4 * hidden + channels]
    w_out_total = matrices[:, 4 * hidden + channels :]
    in_gain_total, in_bias_total, out_gain_total, out_bias_total = vectors
    return (
        pair_grad,
        w_in_total,
        w_gate_total,
        w_out_total,
        in_gain_total,
        in_bias_total,
        out_gain_total,
        out_bias_total,
    )


def solution(mesh):
    fine = Mesh(mesh.devices.reshape(2, 2, 8, 4, 2), ("X", "x", "z", "y", "c"))
    cells = P("X", DAP, None, None)
    in_specs = (
        cells,
        cells,
        P(),
        P(),
        P(),
        P(),
        P(),
        P(),
        P(),
    )
    out_specs = (cells, P(), P(), P(), P(), P(), P(), P())
    return jax.shard_map(
        on_device, mesh=fine, in_specs=in_specs, out_specs=out_specs, check_vma=False
    )
```

```python
import functools

import jax
import jax.numpy as jnp
from jax import lax
from jax.experimental import pallas as pl
from jax.experimental.pallas import tpu as pltpu
from jax.sharding import Mesh, PartitionSpec as P

EPSILON = 1e-05
CHIPS = ("x", "z", "y")
PEERS = ("X", "x", "z", "y")
SWAP = [(0, 1), (1, 0)]
LANES = 128
F32 = jnp.float32
BF16 = jnp.bfloat16


def call(body, outs, scratch=(), work=0):
    def run(*operands):
        return pl.pallas_call(
            body,
            out_shape=[jax.ShapeDtypeStruct(shape, dtype) for shape, dtype in outs],
            in_specs=[pl.BlockSpec(memory_space=pltpu.VMEM)] * len(operands),
            out_specs=[pl.BlockSpec(memory_space=pltpu.VMEM)] * len(outs),
            scratch_shapes=[pltpu.VMEM(shape, F32) for shape in scratch],
            compiler_params=pltpu.CompilerParams(vmem_limit_bytes=24 * 1024 * 1024),
            cost_estimate=pl.CostEstimate(
                flops=work, bytes_accessed=1 << 20, transcendentals=0
            ),
        )(*operands)

    return run


def dot_nt(a, b):
    return lax.dot_general(a, b, (((1,), (1,)), ((), ())), preferred_element_type=F32)


def dot_nn(a, b):
    return lax.dot_general(a, b, (((1,), (0,)), ((), ())), preferred_element_type=F32)


def sigmoid(x):
    return jax.nn.sigmoid(x)


def every(start, count, stride):
    return pl.ds(start, count, stride=stride)


def front(pair_ref, w_in_ref, gain_ref, bias_ref, edges_ref, normed_ref, w_in_t_ref, rows):
    cells, channels = pair_ref.shape
    values = pair_ref[...].astype(F32)
    center = values - jnp.mean(values, axis=1, keepdims=True)
    scale = lax.rsqrt(jnp.mean(center * center, axis=1, keepdims=True) + EPSILON)
    normed = (center * scale * gain_ref[...] + bias_ref[...]).astype(BF16)
    normed_ref[...] = normed
    w_in_t = jnp.transpose(w_in_ref[...].astype(F32)).astype(BF16)
    w_in_t_ref[...] = w_in_t
    hidden = w_in_t.shape[0] // 4
    for side in range(2):
        proj = dot_nt(w_in_t[2 * side * hidden : (2 * side + 1) * hidden], normed)
        gate = dot_nt(w_in_t[(2 * side + 1) * hidden : (2 * side + 2) * hidden], normed)
        value = sigmoid(gate) * proj
        for u in range(4):
            rows[every(4 * side + u, hidden, 8), :] = value[:, u * LANES : (u + 1) * LANES]
    edges_ref[...] = rows[...].astype(BF16)


def beside_front(
    normed_ref, pair_ref, grad_ref, w_in_t_ref, w_gate_ref, w_out_ref, gain_ref,
    normed_t_ref, hat_t_ref, scale_ref, factors_ref, grad_t_ref, gate_t_ref, grad_lin_ref,
    grad_out_normed_ref, scaled_ref, mean_ref,
):
    hidden = w_out_ref.shape[0]
    normed = normed_ref[...]
    normed_t_ref[...] = jnp.transpose(normed.astype(F32)).astype(BF16)
    values = jnp.transpose(pair_ref[...].astype(F32))
    center = values - jnp.mean(values, axis=0, keepdims=True)
    scale = lax.rsqrt(jnp.mean(center * center, axis=0, keepdims=True) + EPSILON)
    hat_t_ref[...] = center * scale
    scale_ref[...] = jnp.broadcast_to(scale, scale_ref.shape)
    grad_t = jnp.transpose(grad_ref[...].astype(F32))
    grad_t_ref[...] = grad_t
    w_gate_t = jnp.transpose(w_gate_ref[...].astype(F32)).astype(BF16)
    gate = sigmoid(dot_nt(w_gate_t, normed))
    gate_t_ref[...] = gate
    grad_lin = (grad_t * gate).astype(BF16)
    grad_lin_ref[...] = grad_lin
    grad_out_normed = dot_nn(w_out_ref[...], grad_lin)
    grad_out_normed_ref[...] = grad_out_normed
    scaled = grad_out_normed * gain_ref[...]
    scaled_ref[...] = scaled
    mean_ref[...] = jnp.broadcast_to(jnp.mean(scaled, axis=0, keepdims=True), mean_ref.shape)
    for side in range(2):
        at = 2 * side * hidden
        proj = dot_nt(w_in_t_ref[at : at + hidden, :], normed)
        sig = sigmoid(dot_nt(w_in_t_ref[at + hidden : at + 2 * hidden, :], normed))
        factors_ref[at : at + hidden, :] = sig
        factors_ref[at + hidden : at + 2 * hidden, :] = proj * sig * (1.0 - sig)


def contract(own_ref, other_ref, product_ref, left_ref, right_ref, own, other, natural, rows):
    core = lax.axis_index("c")
    own[...] = own_ref[...].astype(F32)
    other[...] = other_ref[...].astype(F32)
    chips = own.shape[0] // 16
    for ch in range(2):
        halves = []
        for kh in range(2):
            halves.append(
                jnp.concatenate([own[every(ch * 8 + 2 * r + kh, chips, 16), :] for r in range(2)], axis=0)
            )
            for r in range(2):
                at = every(ch * 8 + 4 + 2 * r + kh, chips, 16)
                mine, theirs = own[at, :], other[at, :]
                base = kh * 4 * chips + r
                natural[every(base, chips, 4), :] = jnp.where(core == 0, mine, theirs)
                natural[every(base + 2, chips, 4), :] = jnp.where(core == 0, theirs, mine)
        left = jnp.concatenate(halves, axis=1).astype(BF16)
        right = jnp.concatenate([natural[: 4 * chips, :], natural[4 * chips :, :]], axis=1).astype(BF16)
        left_ref[ch] = left
        right_ref[ch] = right
        product = dot_nt(left, right)
        for r in range(2):
            for jh in range(2):
                rows[every(ch * 4 + 2 * r + jh, chips, 8), :] = product[
                    r * chips : (r + 1) * chips, jh * LANES : (jh + 1) * LANES
                ]
    product_ref[...] = rows[...].astype(BF16)


def out_norm(values):
    center = values - jnp.mean(values, axis=0, keepdims=True)
    scale = lax.rsqrt(jnp.mean(center * center, axis=0, keepdims=True) + EPSILON)
    return center * scale, scale


def middle(product_ref, scaled_ref, mean_ref, grad_ref, rows, grads):
    hidden = scaled_ref.shape[0]
    rows[...] = product_ref[...].astype(F32)
    for u in range(4):
        hat, scale = out_norm(rows[every(u, hidden, 4), :])
        at = slice(u * LANES, (u + 1) * LANES)
        scaled = scaled_ref[:, at]
        both = jnp.mean(scaled * hat, axis=0, keepdims=True)
        grads[every(u, hidden, 4), :] = scale * (scaled - mean_ref[:1, at] - hat * both)
    grad_ref[...] = grads[...].astype(BF16)


def beside_middle(
    product_ref, grad_out_normed_ref, grad_lin_ref, grad_t_ref, gate_t_ref, normed_t_ref,
    w_out_ref, w_gate_ref, gain_ref, bias_ref, w_out_part_ref, w_gate_part_ref, vectors_ref, gate_term_ref,
    rows,
):
    hidden = w_out_ref.shape[0]
    rows[...] = product_ref[...].astype(F32)
    hats, normed = [], []
    for u in range(4):
        hat, _ = out_norm(rows[every(u, hidden, 4), :])
        hats.append(hat)
        normed.append((hat * gain_ref[...] + bias_ref[...]).astype(BF16))
    hat = jnp.concatenate(hats, axis=1)
    out_normed = jnp.concatenate(normed, axis=1)
    w_out_t = jnp.transpose(w_out_ref[...].astype(F32)).astype(BF16)
    outlin = dot_nn(w_out_t, out_normed)
    gate = gate_t_ref[...]
    grad_gate = (grad_t_ref[...] * outlin * gate * (1.0 - gate)).astype(BF16)
    w_out_part_ref[...] = dot_nt(out_normed, grad_lin_ref[...])
    w_gate_part_ref[...] = dot_nt(normed_t_ref[...], grad_gate)
    gate_term_ref[...] = dot_nn(w_gate_ref[...], grad_gate)
    grad_out_normed = grad_out_normed_ref[...]
    vectors_ref[...] = columns(
        jnp.sum(grad_out_normed * hat, axis=1, keepdims=True),
        jnp.sum(grad_out_normed, axis=1, keepdims=True),
    )


def columns(first, second):
    lane = lax.broadcasted_iota(jnp.int32, (first.shape[0], LANES), 1)
    return jnp.where(lane == 0, first, jnp.where(lane == 1, second, 0.0))


def contract_back(grad_ref, left_ref, right_ref, grad_left_ref, keep_ref, give_ref, rows, natural):
    core = lax.axis_index("c")
    rows[...] = grad_ref[...].astype(F32)
    chips = rows.shape[0] // 8
    pieces = []
    for ch in range(2):
        halves = []
        for jh in range(2):
            halves.append(
                jnp.concatenate([rows[every(ch * 4 + 2 * r + jh, chips, 8), :] for r in range(2)], axis=0)
            )
        grad = jnp.concatenate(halves, axis=1)
        grad_t = jnp.transpose(grad).astype(BF16)
        grad_right = dot_nn(grad_t, left_ref[ch])
        natural[: 4 * chips, :] = grad_right[:, :LANES]
        natural[4 * chips :, :] = grad_right[:, LANES:]
        for r in range(2):
            for kh in range(2):
                base = kh * 4 * chips + r
                low = natural[every(base, chips, 4), :]
                high = natural[every(base + 2, chips, 4), :]
                at = every(ch * 4 + 2 * r + kh, chips, 8)
                keep_ref[at, :] = jnp.where(core == 0, low, high)
                give_ref[at, :] = jnp.where(core == 0, high, low)
        pieces.append(dot_nn(grad.astype(BF16), right_ref[ch]))
    for ch in range(2):
        for r in range(2):
            for kh in range(2):
                rows[every(ch * 4 + 2 * r + kh, chips, 8), :] = pieces[ch][
                    r * chips : (r + 1) * chips, kh * LANES : (kh + 1) * LANES
                ]
    grad_left_ref[...] = rows[...]


def join(grad_left_ref, keep_ref, got_ref, edges_ref):
    grad_left = grad_left_ref[...].reshape(-1, 8, LANES)
    grad_right = (keep_ref[...] + got_ref[...]).reshape(-1, 8, LANES)
    both = jnp.concatenate([grad_left, grad_right], axis=1)
    edges_ref[...] = both.reshape(-1, LANES).astype(BF16)


def rear(
    edges_ref, factors_ref, normed_t_ref, hat_t_ref, w_in_ref, gate_term_ref, w_out_part_ref, w_gate_part_ref,
    vectors_ref, keep_ref, give_ref, grad_normed_ref, lefts, rights, low, high,
):
    core = lax.axis_index("c")
    hidden = w_in_ref.shape[1] // 4
    edges = edges_ref[...].astype(F32).reshape(-1, 16, LANES)
    lefts[...] = edges[:, :8, :].reshape(-1, LANES)
    rights[...] = edges[:, 8:, :].reshape(-1, LANES)
    parts = []
    for u in range(4):
        at = slice(u * LANES, (u + 1) * LANES)
        left = lefts[every(u, hidden, 4), :]
        right = rights[every(u, hidden, 4), :]
        parts.append(
            jnp.concatenate(
                [
                    left * factors_ref[:hidden, at],
                    left * factors_ref[hidden : 2 * hidden, at],
                    right * factors_ref[2 * hidden : 3 * hidden, at],
                    right * factors_ref[3 * hidden :, at],
                ],
                axis=0,
            ).astype(BF16)
        )
    grad_projected = jnp.concatenate(parts, axis=1)
    w_in_part = dot_nt(normed_t_ref[...], grad_projected)
    grad_normed = dot_nn(w_in_ref[...], grad_projected) + gate_term_ref[...]
    grad_normed_ref[...] = grad_normed
    channels = w_in_part.shape[0]
    for t in range(3):
        low[every(t, channels, 4), :] = w_in_part[:, t * LANES : (t + 1) * LANES]
    low[every(3, channels, 4), :] = columns(
        jnp.sum(grad_normed * hat_t_ref[...], axis=1, keepdims=True),
        jnp.sum(grad_normed, axis=1, keepdims=True),
    )
    high[every(0, channels, 4), :] = w_in_part[:, 3 * LANES :]
    high[every(1, channels, 4), :] = w_gate_part_ref[...]
    high[every(2, channels, 4), :] = w_out_part_ref[...]
    high[every(3, channels, 4), :] = vectors_ref[...]
    keep_ref[...] = jnp.where(core == 0, low[...], high[...])
    give_ref[...] = jnp.where(core == 0, high[...], low[...])


def beside_rear(grad_normed_ref, hat_t_ref, scale_ref, gain_ref, pair_grad_ref):
    hat = hat_t_ref[...]
    scaled = grad_normed_ref[...] * gain_ref[...]
    grad = scale_ref[:1, :] * (
        scaled
        - jnp.mean(scaled, axis=0, keepdims=True)
        - hat * jnp.mean(scaled * hat, axis=0, keepdims=True)
    )
    pair_grad_ref[...] = jnp.transpose(grad).astype(BF16)


def add(keep_ref, got_ref, sum_ref):
    sum_ref[...] = keep_ref[...] + got_ref[...]


def reduce_share(parts_ref, share_ref):
    total = jnp.sum(parts_ref[...].reshape(-1, 8, LANES), axis=0)
    total = total[:4] + total[4:]
    both = jnp.concatenate([total, total], axis=0)
    share_ref[...] = (
        jnp.broadcast_to(both[None], (share_ref.shape[0] // 8, 8, LANES))
        .reshape(share_ref.shape)
        .astype(BF16)
    )


def finish(own_ref, other_ref, w_in_ref, w_gate_ref, w_out_ref, vectors_ref, low, high):
    core = lax.axis_index("c")
    own, other = own_ref[...].astype(F32), other_ref[...].astype(F32)
    low[...] = jnp.where(core == 0, own, other)
    high[...] = jnp.where(core == 0, other, own)
    channels = w_in_ref.shape[0]
    for t in range(3):
        w_in_ref[:, t * LANES : (t + 1) * LANES] = low[every(t, channels, 4), :]
    w_in_ref[:, 3 * LANES :] = high[every(0, channels, 4), :]
    w_gate_ref[...] = high[every(1, channels, 4), :]
    w_out_ref[...] = high[every(2, channels, 4), :]
    inner = jnp.transpose(low[every(3, channels, 4), :])
    outer = jnp.transpose(high[every(3, channels, 4), :])
    vectors_ref[...] = jnp.concatenate([inner[:2], outer[:2], inner[:2], outer[:2]], axis=0)


def on_device(
    pair, grad_out, w_in, w_gate, w_out, ln_in_gain, ln_in_bias, ln_out_gain, ln_out_bias
):
    shape = pair.shape
    channels = shape[3]
    hidden = w_out.shape[0]
    cells = shape[1] * shape[2]
    full_len = shape[2]
    pair2 = pair.reshape(cells, channels)
    grad2 = grad_out.reshape(cells, channels)
    in_gain_row, in_bias_row = ln_in_gain.reshape(1, -1), ln_in_bias.reshape(1, -1)
    in_gain_col = ln_in_gain.reshape(-1, 1)
    out_gain_col, out_bias_col = ln_out_gain.reshape(-1, 1), ln_out_bias.reshape(-1, 1)
    grid = (hidden, cells)
    quarter = (4 * hidden, LANES)
    whole = (8 * hidden, LANES)
    flat = lambda axes: lambda a: lax.all_to_all(a, axes, 0, 0, tiled=True)
    to_chips, to_peers = flat(CHIPS), flat(PEERS)
    swap = lambda a: lax.ppermute(a, "c", SWAP)

    edges, normed, w_in_t = call(
        front, [(whole, BF16), ((cells, channels), BF16), ((4 * hidden, channels), BF16)], [whole]
    )(pair2, w_in, in_gain_row, in_bias_row)
    own = to_chips(edges)
    normed_t, hat_t, scale, factors, grad_t, gate_t, grad_lin, grad_out_normed, scaled, mean = call(
        beside_front,
        [
            (grid, BF16), (grid, F32), ((8, cells), F32), ((4 * hidden, cells), F32), (grid, F32), (grid, F32),
            (grid, BF16), (grid, F32), (grid, F32), ((8, cells), F32),
        ],
        work=1 << 28,
    )(normed, pair2, grad2, w_in_t, w_gate, w_out, out_gain_col)
    other = swap(own)
    product, left, right = call(
        contract,
        [(quarter, BF16), ((2, full_len // 2, full_len), BF16), ((2, full_len, full_len), BF16)],
        [whole, whole, quarter, quarter],
    )(own, other)
    product = to_chips(product)
    (grad_product,) = call(middle, [(quarter, BF16)], [quarter, quarter])(product, scaled, mean)
    grad_cols = to_chips(grad_product)
    w_out_part, w_gate_part, vectors, gate_term = call(
        beside_middle,
        [((hidden, channels), F32), ((channels, channels), F32), ((hidden, LANES), F32), (grid, F32)],
        [quarter],
        work=1 << 28,
    )(product, grad_out_normed, grad_lin, grad_t, gate_t, normed_t, w_out, w_gate, out_gain_col, out_bias_col)
    grad_left, keep, give = call(contract_back, [(quarter, F32)] * 3, [quarter, quarter])(
        grad_cols, left, right
    )
    (grad_edges,) = call(join, [(whole, BF16)])(grad_left, keep, swap(give))
    grad_edges = to_chips(grad_edges)
    keep, give, grad_normed = call(
        rear, [(quarter, F32), (quarter, F32), (grid, F32)], [quarter] * 4
    )(grad_edges, factors, normed_t, hat_t, w_in, gate_term, w_out_part, w_gate_part, vectors)
    (parts,) = call(add, [(quarter, F32)])(keep, swap(give))
    parts = to_peers(parts)
    (pair_grad,) = call(beside_rear, [((cells, channels), BF16)], work=1 << 28)(
        grad_normed, hat_t, scale, in_gain_col
    )
    (share,) = call(reduce_share, [(quarter, BF16)])(parts)
    mine = to_peers(share)
    w_in_total, w_gate_total, w_out_total, vectors = call(
        finish,
        [(w_in.shape, F32), (w_gate.shape, F32), (w_out.shape, F32), ((8, LANES), F32)],
        [quarter, quarter],
    )(mine, swap(mine))
    return (
        pair_grad.reshape(shape),
        w_in_total,
        w_gate_total,
        w_out_total,
        vectors[0],
        vectors[1],
        vectors[2],
        vectors[3],
    )


def solution(mesh):
    fine = Mesh(mesh.devices.reshape(2, 2, 8, 4, 2), ("X", "x", "z", "y", "c"))
    cells = P("X", ("x", "z", "y", "c"), None, None)
    in_specs = (cells, cells, P(), P(), P(), P(), P(), P(), P())
    out_specs = (cells, P(), P(), P(), P(), P(), P(), P())
    return jax.shard_map(
        on_device, mesh=fine, in_specs=in_specs, out_specs=out_specs, check_vma=False
    )
```

```python
import functools

import jax
import jax.numpy as jnp
from jax import lax
from jax.experimental import pallas as pl
from jax.experimental.pallas import tpu as pltpu
from jax.sharding import Mesh, PartitionSpec as P

EPSILON = 1e-05
CHIPS = ("x", "z", "y")
PEERS = ("X", "x", "z", "y")
SWAP = [(0, 1), (1, 0)]
LANES = 128
F32 = jnp.float32
BF16 = jnp.bfloat16


def call(body, outs, scratch=(), work=0, far=0):
    def run(*operands):
        return pl.pallas_call(
            body,
            out_shape=[jax.ShapeDtypeStruct(shape, dtype) for shape, dtype in outs],
            in_specs=[pl.BlockSpec(memory_space=pltpu.HBM)] * far
            + [pl.BlockSpec(memory_space=pltpu.VMEM)] * (len(operands) - far),
            out_specs=[pl.BlockSpec(memory_space=pltpu.VMEM)] * len(outs),
            scratch_shapes=[pltpu.VMEM(s, F32) if isinstance(s, tuple) else s for s in scratch],
            compiler_params=pltpu.CompilerParams(vmem_limit_bytes=8 * 1024 * 1024),
            cost_estimate=pl.CostEstimate(
                flops=work, bytes_accessed=1 << 20, transcendentals=0
            ),
        )(*operands)

    return run


def dot_nt(a, b):
    return lax.dot_general(a, b, (((1,), (1,)), ((), ())), preferred_element_type=F32)


def dot_nn(a, b):
    return lax.dot_general(a, b, (((1,), (0,)), ((), ())), preferred_element_type=F32)


def sigmoid(x):
    return jax.nn.sigmoid(x)


def every(start, count, stride):
    return pl.ds(start, count, stride=stride)


def column(row):
    return jnp.transpose(jnp.broadcast_to(row, (LANES, row.shape[1])))[:, :1]


def front(
    pair_far, w_in_far, gain_far, bias_far, edges_ref, normed_ref, w_in_t_ref,
    rows, pair_ref, w_in_ref, gain_ref, bias_ref, arrived,
):
    copies = [
        pltpu.make_async_copy(source, target, arrived.at[n])
        for n, (source, target) in enumerate(
            [(pair_far, pair_ref), (gain_far, gain_ref), (bias_far, bias_ref), (w_in_far, w_in_ref)]
        )
    ]
    for copy in copies:
        copy.start()
    for copy in copies:
        copy.wait()
    values = pair_ref[...].astype(F32)
    center = values - jnp.mean(values, axis=1, keepdims=True)
    scale = lax.rsqrt(jnp.mean(center * center, axis=1, keepdims=True) + EPSILON)
    normed = (center * scale * gain_ref[...] + bias_ref[...]).astype(BF16)
    normed_ref[...] = normed
    w_in_t = jnp.transpose(w_in_ref[...].astype(F32)).astype(BF16)
    w_in_t_ref[...] = w_in_t
    hidden = w_in_t.shape[0] // 4
    for side in range(2):
        proj = dot_nt(w_in_t[2 * side * hidden : (2 * side + 1) * hidden], normed)
        gate = dot_nt(w_in_t[(2 * side + 1) * hidden : (2 * side + 2) * hidden], normed)
        value = sigmoid(gate) * proj
        for u in range(4):
            rows[every(4 * side + u, hidden, 8), :] = value[:, u * LANES : (u + 1) * LANES]
    edges_ref[...] = rows[...].astype(BF16)


def beside_front(
    normed_ref, pair_ref, grad_ref, w_in_t_ref, w_gate_ref, w_out_ref, gain_ref,
    normed_t_ref, hat_t_ref, scale_ref, factors_ref, grad_t_ref, gate_t_ref, grad_lin_ref,
    grad_out_normed_ref, scaled_ref, mean_ref,
):
    hidden = w_out_ref.shape[0]
    normed = normed_ref[...]
    normed_t_ref[...] = jnp.transpose(normed.astype(F32)).astype(BF16)
    values = jnp.transpose(pair_ref[...].astype(F32))
    center = values - jnp.mean(values, axis=0, keepdims=True)
    scale = lax.rsqrt(jnp.mean(center * center, axis=0, keepdims=True) + EPSILON)
    hat_t_ref[...] = center * scale
    scale_ref[...] = jnp.broadcast_to(scale, scale_ref.shape)
    grad_t = jnp.transpose(grad_ref[...].astype(F32))
    grad_t_ref[...] = grad_t
    w_gate_t = jnp.transpose(w_gate_ref[...].astype(F32)).astype(BF16)
    gate = sigmoid(dot_nt(w_gate_t, normed))
    gate_t_ref[...] = gate
    grad_lin = (grad_t * gate).astype(BF16)
    grad_lin_ref[...] = grad_lin
    grad_out_normed = dot_nn(w_out_ref[...], grad_lin)
    grad_out_normed_ref[...] = grad_out_normed
    scaled = grad_out_normed * column(gain_ref[...])
    scaled_ref[...] = scaled
    mean_ref[...] = jnp.broadcast_to(jnp.mean(scaled, axis=0, keepdims=True), mean_ref.shape)
    for side in range(2):
        at = 2 * side * hidden
        proj = dot_nt(w_in_t_ref[at : at + hidden, :], normed)
        sig = sigmoid(dot_nt(w_in_t_ref[at + hidden : at + 2 * hidden, :], normed))
        factors_ref[at : at + hidden, :] = sig
        factors_ref[at + hidden : at + 2 * hidden, :] = proj * sig * (1.0 - sig)


def contract(own_ref, other_ref, product_ref, left_ref, right_ref, own, other, natural, rows):
    core = lax.axis_index("c")
    own[...] = own_ref[...].astype(F32)
    other[...] = other_ref[...].astype(F32)
    chips = own.shape[0] // 16
    for ch in range(2):
        halves = []
        for kh in range(2):
            halves.append(
                jnp.concatenate([own[every(ch * 8 + 2 * r + kh, chips, 16), :] for r in range(2)], axis=0)
            )
            for r in range(2):
                at = every(ch * 8 + 4 + 2 * r + kh, chips, 16)
                mine, theirs = own[at, :], other[at, :]
                base = kh * 4 * chips + r
                natural[every(base, chips, 4), :] = jnp.where(core == 0, mine, theirs)
                natural[every(base + 2, chips, 4), :] = jnp.where(core == 0, theirs, mine)
        left = jnp.concatenate(halves, axis=1).astype(BF16)
        right = jnp.concatenate([natural[: 4 * chips, :], natural[4 * chips :, :]], axis=1).astype(BF16)
        left_ref[ch] = left
        right_ref[ch] = right
        product = dot_nt(left, right)
        for r in range(2):
            for jh in range(2):
                rows[every(ch * 4 + 2 * r + jh, chips, 8), :] = product[
                    r * chips : (r + 1) * chips, jh * LANES : (jh + 1) * LANES
                ]
    product_ref[...] = rows[...].astype(BF16)


def out_norm(values):
    center = values - jnp.mean(values, axis=0, keepdims=True)
    scale = lax.rsqrt(jnp.mean(center * center, axis=0, keepdims=True) + EPSILON)
    return center * scale, scale


def middle(product_ref, scaled_ref, mean_ref, grad_ref, rows, grads):
    hidden = scaled_ref.shape[0]
    rows[...] = product_ref[...].astype(F32)
    for u in range(4):
        hat, scale = out_norm(rows[every(u, hidden, 4), :])
        at = slice(u * LANES, (u + 1) * LANES)
        scaled = scaled_ref[:, at]
        both = jnp.mean(scaled * hat, axis=0, keepdims=True)
        grads[every(u, hidden, 4), :] = scale * (scaled - mean_ref[:1, at] - hat * both)
    grad_ref[...] = grads[...].astype(BF16)


def beside_middle(
    product_ref, grad_out_normed_ref, grad_lin_ref, grad_t_ref, gate_t_ref, normed_t_ref,
    w_out_ref, w_gate_ref, gain_ref, bias_ref, w_out_part_ref, w_gate_part_ref, vectors_ref, gate_term_ref,
    rows,
):
    hidden = w_out_ref.shape[0]
    rows[...] = product_ref[...].astype(F32)
    hats, normed = [], []
    gain, bias = column(gain_ref[...]), column(bias_ref[...])
    for u in range(4):
        hat, _ = out_norm(rows[every(u, hidden, 4), :])
        hats.append(hat)
        normed.append((hat * gain + bias).astype(BF16))
    hat = jnp.concatenate(hats, axis=1)
    out_normed = jnp.concatenate(normed, axis=1)
    w_out_t = jnp.transpose(w_out_ref[...].astype(F32)).astype(BF16)
    outlin = dot_nn(w_out_t, out_normed)
    gate = gate_t_ref[...]
    grad_gate = (grad_t_ref[...] * outlin * gate * (1.0 - gate)).astype(BF16)
    w_out_part_ref[...] = dot_nt(out_normed, grad_lin_ref[...])
    w_gate_part_ref[...] = dot_nt(normed_t_ref[...], grad_gate)
    gate_term_ref[...] = dot_nn(w_gate_ref[...], grad_gate)
    grad_out_normed = grad_out_normed_ref[...]
    vectors_ref[...] = columns(
        jnp.sum(grad_out_normed * hat, axis=1, keepdims=True),
        jnp.sum(grad_out_normed, axis=1, keepdims=True),
    )


def columns(*sums):
    lane = lax.broadcasted_iota(jnp.int32, (sums[0].shape[0], LANES), 1)
    high = [value.astype(BF16).astype(F32) for value in sums]
    out = jnp.zeros(lane.shape, F32)
    for n, value in enumerate(high + [value - top for value, top in zip(sums, high)]):
        out = jnp.where(lane == n, value, out)
    return out


def contract_back(grad_ref, left_ref, right_ref, grad_left_ref, keep_ref, give_ref, rows, natural):
    core = lax.axis_index("c")
    rows[...] = grad_ref[...].astype(F32)
    chips = rows.shape[0] // 8
    pieces = []
    for ch in range(2):
        halves = []
        for jh in range(2):
            halves.append(
                jnp.concatenate([rows[every(ch * 4 + 2 * r + jh, chips, 8), :] for r in range(2)], axis=0)
            )
        grad = jnp.concatenate(halves, axis=1)
        grad_t = jnp.transpose(grad).astype(BF16)
        grad_right = dot_nn(grad_t, left_ref[ch])
        natural[: 4 * chips, :] = grad_right[:, :LANES]
        natural[4 * chips :, :] = grad_right[:, LANES:]
        for r in range(2):
            for kh in range(2):
                base = kh * 4 * chips + r
                low = natural[every(base, chips, 4), :]
                high = natural[every(base + 2, chips, 4), :]
                at = every(ch * 4 + 2 * r + kh, chips, 8)
                keep_ref[at, :] = jnp.where(core == 0, low, high)
                give_ref[at, :] = jnp.where(core == 0, high, low)
        pieces.append(dot_nn(grad.astype(BF16), right_ref[ch]))
    for ch in range(2):
        for r in range(2):
            for kh in range(2):
                rows[every(ch * 4 + 2 * r + kh, chips, 8), :] = pieces[ch][
                    r * chips : (r + 1) * chips, kh * LANES : (kh + 1) * LANES
                ]
    grad_left_ref[...] = rows[...]


def join(grad_left_ref, keep_ref, got_ref, edges_ref):
    grad_left = grad_left_ref[...].reshape(-1, 8, LANES)
    grad_right = (keep_ref[...] + got_ref[...]).reshape(-1, 8, LANES)
    both = jnp.concatenate([grad_left, grad_right], axis=1)
    edges_ref[...] = both.reshape(-1, LANES).astype(BF16)


def rear(
    edges_ref, factors_ref, normed_t_ref, hat_t_ref, w_in_ref, gate_term_ref, w_out_part_ref, w_gate_part_ref,
    vectors_ref, keep_ref, give_ref, grad_normed_ref, lefts, rights, low, high,
):
    core = lax.axis_index("c")
    hidden = w_in_ref.shape[1] // 4
    edges = edges_ref[...].astype(F32).reshape(-1, 16, LANES)
    lefts[...] = edges[:, :8, :].reshape(-1, LANES)
    rights[...] = edges[:, 8:, :].reshape(-1, LANES)
    parts = []
    for u in range(4):
        at = slice(u * LANES, (u + 1) * LANES)
        left = lefts[every(u, hidden, 4), :]
        right = rights[every(u, hidden, 4), :]
        parts.append(
            jnp.concatenate(
                [
                    left * factors_ref[:hidden, at],
                    left * factors_ref[hidden : 2 * hidden, at],
                    right * factors_ref[2 * hidden : 3 * hidden, at],
                    right * factors_ref[3 * hidden :, at],
                ],
                axis=0,
            ).astype(BF16)
        )
    grad_projected = jnp.concatenate(parts, axis=1)
    w_in_part = dot_nt(normed_t_ref[...], grad_projected)
    grad_normed = dot_nn(w_in_ref[...], grad_projected) + gate_term_ref[...]
    grad_normed_ref[...] = grad_normed
    channels = w_in_part.shape[0]
    for t in range(3):
        low[every(t, channels, 4), :] = w_in_part[:, t * LANES : (t + 1) * LANES]
    low[every(3, channels, 4), :] = columns(
        jnp.sum(grad_normed * hat_t_ref[...], axis=1, keepdims=True),
        jnp.sum(grad_normed, axis=1, keepdims=True),
    )
    high[every(0, channels, 4), :] = w_in_part[:, 3 * LANES :]
    high[every(1, channels, 4), :] = w_gate_part_ref[...]
    high[every(2, channels, 4), :] = w_out_part_ref[...]
    high[every(3, channels, 4), :] = vectors_ref[...]
    keep_ref[...] = jnp.where(core == 0, low[...], high[...])
    give_ref[...] = jnp.where(core == 0, high[...], low[...])


def beside_rear(grad_normed_ref, hat_t_ref, scale_ref, gain_ref, pair_grad_ref):
    hat = hat_t_ref[...]
    scaled = grad_normed_ref[...] * column(gain_ref[...])
    grad = scale_ref[:1, :] * (
        scaled
        - jnp.mean(scaled, axis=0, keepdims=True)
        - hat * jnp.mean(scaled * hat, axis=0, keepdims=True)
    )
    pair_grad_ref[...] = jnp.transpose(grad).astype(BF16)


def split_vectors(values):
    lane = lax.broadcasted_iota(jnp.int32, values.shape, values.ndim - 1)
    row = lax.broadcasted_iota(jnp.int32, values.shape, values.ndim - 2)
    total = values + pltpu.roll(values, LANES - 2, values.ndim - 1)
    high = total.astype(BF16).astype(F32)
    low = pltpu.roll(total - high, 2, values.ndim - 1)
    return jnp.where(row % 4 == 3, jnp.where(lane < 2, high, jnp.where(lane < 4, low, 0.0)), values)


def add(keep_ref, got_ref, sum_ref):
    sum_ref[...] = split_vectors(keep_ref[...] + got_ref[...]).astype(BF16)


def reduce_share(parts_ref, share_ref):
    total = jnp.sum(parts_ref[...].astype(F32).reshape(-1, 8, LANES), axis=0)
    total = total[:4] + total[4:]
    both = split_vectors(jnp.concatenate([total, total], axis=0))
    share_ref[...] = (
        jnp.broadcast_to(both[None], (share_ref.shape[0] // 8, 8, LANES))
        .reshape(share_ref.shape)
        .astype(BF16)
    )


def finish(
    own_ref, other_ref, w_in_ref, w_gate_ref, w_out_ref, in_gain_ref, in_bias_ref, out_gain_ref, out_bias_ref, low, high
):
    core = lax.axis_index("c")
    own, other = own_ref[...].astype(F32), other_ref[...].astype(F32)
    low[...] = jnp.where(core == 0, own, other)
    high[...] = jnp.where(core == 0, other, own)
    channels = w_in_ref.shape[0]
    for t in range(3):
        w_in_ref[:, t * LANES : (t + 1) * LANES] = low[every(t, channels, 4), :]
    w_in_ref[:, 3 * LANES :] = high[every(0, channels, 4), :]
    w_gate_ref[...] = high[every(1, channels, 4), :]
    w_out_ref[...] = high[every(2, channels, 4), :]
    inner = jnp.transpose(low[every(3, channels, 4), :])
    outer = jnp.transpose(high[every(3, channels, 4), :])
    inner, outer = inner[:2] + inner[2:4], outer[:2] + outer[2:4]
    in_gain_ref[...], in_bias_ref[...] = inner[:1], inner[1:2]
    out_gain_ref[...], out_bias_ref[...] = outer[:1], outer[1:2]


def on_device(
    pair, grad_out, w_in, w_gate, w_out, ln_in_gain, ln_in_bias, ln_out_gain, ln_out_bias
):
    shape = pair.shape
    channels = shape[3]
    hidden = w_out.shape[0]
    cells = shape[1] * shape[2]
    full_len = shape[2]
    pair2 = pair.reshape(cells, channels)
    grad2 = grad_out.reshape(cells, channels)
    in_gain_row, in_bias_row = ln_in_gain.reshape(1, -1), ln_in_bias.reshape(1, -1)
    out_gain_row, out_bias_row = ln_out_gain.reshape(1, -1), ln_out_bias.reshape(1, -1)
    grid = (hidden, cells)
    quarter = (4 * hidden, LANES)
    whole = (8 * hidden, LANES)
    flat = lambda axes: lambda a: lax.all_to_all(a, axes, 0, 0, tiled=True)
    to_chips, to_peers = flat(CHIPS), flat(PEERS)
    swap = lambda a: lax.ppermute(a, "c", SWAP)

    edges, normed, w_in_t = call(
        front, [(whole, BF16), ((cells, channels), BF16), ((4 * hidden, channels), BF16)],
        [
            whole, pltpu.VMEM((cells, channels), BF16), pltpu.VMEM(w_in.shape, BF16), (1, channels), (1, channels),
            pltpu.SemaphoreType.DMA((4,)),
        ],
        far=4,
    )(pair2, w_in, in_gain_row, in_bias_row)
    own, normed = lax.optimization_barrier((to_chips(edges), normed))
    other = swap(own)
    normed_t, hat_t, scale, factors, grad_t, gate_t, grad_lin, grad_out_normed, scaled, mean = call(
        beside_front,
        [
            (grid, BF16), (grid, F32), ((8, cells), F32), ((4 * hidden, cells), F32), (grid, F32), (grid, F32),
            (grid, BF16), (grid, F32), (grid, F32), ((8, cells), F32),
        ],
        work=1 << 28,
    )(normed, pair2, grad2, w_in_t, w_gate, w_out, out_gain_row)
    other, normed_t = lax.optimization_barrier((other, normed_t))
    product, left, right = call(
        contract,
        [(quarter, BF16), ((2, full_len // 2, full_len), BF16), ((2, full_len, full_len), BF16)],
        [whole, whole, quarter, quarter],
    )(own, other)
    product = to_chips(product)
    (grad_product,) = call(middle, [(quarter, BF16)], [quarter, quarter])(product, scaled, mean)
    grad_cols = to_chips(grad_product)
    grad_left, keep, give = call(contract_back, [(quarter, F32)] * 3, [quarter, quarter])(
        grad_cols, left, right
    )
    give, product = lax.optimization_barrier((give, product))
    got = swap(give)
    w_out_part, w_gate_part, vectors, gate_term = call(
        beside_middle,
        [((hidden, channels), F32), ((channels, channels), F32), ((hidden, LANES), F32), (grid, F32)],
        [quarter],
        work=1 << 28,
    )(product, grad_out_normed, grad_lin, grad_t, gate_t, normed_t, w_out, w_gate, out_gain_row, out_bias_row)
    got, vectors = lax.optimization_barrier((got, vectors))
    (grad_edges,) = call(join, [(whole, BF16)])(grad_left, keep, got)
    grad_edges = to_chips(grad_edges)
    keep, give, grad_normed = call(
        rear, [(quarter, F32), (quarter, F32), (grid, F32)], [quarter] * 4
    )(grad_edges, factors, normed_t, hat_t, w_in, gate_term, w_out_part, w_gate_part, vectors)
    got = swap(give)
    (pair_grad,) = call(beside_rear, [((cells, channels), BF16)], work=1 << 28)(
        grad_normed, hat_t, scale, in_gain_row
    )
    got, pair_grad = lax.optimization_barrier((got, pair_grad))
    (parts,) = call(add, [(quarter, BF16)])(keep, got)
    parts = to_peers(parts)
    (share,) = call(reduce_share, [(quarter, BF16)])(parts)
    mine = to_peers(share)
    w_in_total, w_gate_total, w_out_total, *vectors = call(
        finish,
        [(w_in.shape, F32), (w_gate.shape, F32), (w_out.shape, F32)] + [((1, LANES), F32)] * 4,
        [quarter, quarter],
    )(mine, swap(mine))
    return (
        pair_grad.reshape(shape),
        w_in_total,
        w_gate_total,
        w_out_total,
        *(vector.reshape(-1) for vector in vectors),
    )


def solution(mesh):
    fine = Mesh(mesh.devices.reshape(2, 2, 8, 4, 2), ("X", "x", "z", "y", "c"))
    cells = P("X", ("x", "z", "y", "c"), None, None)
    in_specs = (cells, cells, P(), P(), P(), P(), P(), P(), P())
    out_specs = (cells, P(), P(), P(), P(), P(), P(), P())
    return jax.shard_map(
        on_device, mesh=fine, in_specs=in_specs, out_specs=out_specs, check_vma=False
    )
```

```python
import functools

import jax
import jax.numpy as jnp
from jax import lax
from jax.experimental import pallas as pl
from jax.experimental.pallas import tpu as pltpu
from jax.sharding import Mesh, PartitionSpec as P

EPSILON = 1e-05
CHIPS = ("x", "z", "y")
PEERS = ("X", "x", "z", "y")
SWAP = [(0, 1), (1, 0)]
LANES = 128
F32 = jnp.float32
BF16 = jnp.bfloat16


def call(body, outs, scratch=(), work=0, far=0):
    def run(*operands):
        return pl.pallas_call(
            body,
            out_shape=[jax.ShapeDtypeStruct(shape, dtype) for shape, dtype in outs],
            in_specs=[pl.BlockSpec(memory_space=pltpu.HBM)] * far
            + [pl.BlockSpec(memory_space=pltpu.VMEM)] * (len(operands) - far),
            out_specs=[pl.BlockSpec(memory_space=pltpu.VMEM)] * len(outs),
            scratch_shapes=[pltpu.VMEM(s, F32) if isinstance(s, tuple) else s for s in scratch],
            compiler_params=pltpu.CompilerParams(vmem_limit_bytes=8 * 1024 * 1024),
            cost_estimate=pl.CostEstimate(
                flops=work, bytes_accessed=1 << 20, transcendentals=0
            ),
        )(*operands)

    return run


def dot_nt(a, b):
    return lax.dot_general(a, b, (((1,), (1,)), ((), ())), preferred_element_type=F32)


def dot_nn(a, b):
    return lax.dot_general(a, b, (((1,), (0,)), ((), ())), preferred_element_type=F32)


def sigmoid(x):
    return jax.nn.sigmoid(x)


def every(start, count, stride):
    return pl.ds(start, count, stride=stride)


def column(row):
    return jnp.transpose(jnp.broadcast_to(row, (LANES, row.shape[1])))[:, :1]


def front(
    pair_far, gain_far, bias_far, w_in_far, edges_ref, normed_ref, w_in_t_ref,
    rows, pair_ref, w_in_ref, gain_ref, bias_ref, arrived,
):
    copies = [
        pltpu.make_async_copy(source, target, arrived.at[n])
        for n, (source, target) in enumerate(
            [(pair_far, pair_ref), (gain_far, gain_ref), (bias_far, bias_ref), (w_in_far, w_in_ref)]
        )
    ]
    for copy in copies:
        copy.start()
    for copy in copies[:3]:
        copy.wait()
    values = pair_ref[...].astype(F32)
    center = values - jnp.mean(values, axis=1, keepdims=True)
    scale = lax.rsqrt(jnp.mean(center * center, axis=1, keepdims=True) + EPSILON)
    normed = (center * scale * gain_ref[...] + bias_ref[...]).astype(BF16)
    normed_ref[...] = normed
    copies[3].wait()
    w_in_t = jnp.transpose(w_in_ref[...].astype(F32)).astype(BF16)
    w_in_t_ref[...] = w_in_t
    hidden = w_in_t.shape[0] // 4
    for side in range(2):
        proj = dot_nt(w_in_t[2 * side * hidden : (2 * side + 1) * hidden], normed)
        gate = dot_nt(w_in_t[(2 * side + 1) * hidden : (2 * side + 2) * hidden], normed)
        value = sigmoid(gate) * proj
        for u in range(4):
            rows[every(4 * side + u, hidden, 8), :] = value[:, u * LANES : (u + 1) * LANES]
    edges_ref[...] = rows[...].astype(BF16)


def beside_front(
    normed_ref, pair_ref, grad_ref, w_in_t_ref, w_gate_ref, w_out_ref, gain_ref,
    normed_t_ref, hat_t_ref, scale_ref, factors_ref, grad_t_ref, gate_t_ref, grad_lin_ref,
    grad_out_normed_ref, scaled_ref, mean_ref,
):
    hidden = w_out_ref.shape[0]
    normed = normed_ref[...]
    normed_t_ref[...] = jnp.transpose(normed.astype(F32)).astype(BF16)
    values = jnp.transpose(pair_ref[...].astype(F32))
    center = values - jnp.mean(values, axis=0, keepdims=True)
    scale = lax.rsqrt(jnp.mean(center * center, axis=0, keepdims=True) + EPSILON)
    hat_t_ref[...] = center * scale
    scale_ref[...] = jnp.broadcast_to(scale, scale_ref.shape)
    grad_t = jnp.transpose(grad_ref[...].astype(F32))
    grad_t_ref[...] = grad_t
    w_gate_t = jnp.transpose(w_gate_ref[...].astype(F32)).astype(BF16)
    gate = sigmoid(dot_nt(w_gate_t, normed))
    gate_t_ref[...] = gate
    grad_lin = (grad_t * gate).astype(BF16)
    grad_lin_ref[...] = grad_lin
    grad_out_normed = dot_nn(w_out_ref[...], grad_lin)
    grad_out_normed_ref[...] = grad_out_normed
    scaled = grad_out_normed * column(gain_ref[...])
    scaled_ref[...] = scaled
    mean_ref[...] = jnp.broadcast_to(jnp.mean(scaled, axis=0, keepdims=True), mean_ref.shape)
    for side in range(2):
        at = 2 * side * hidden
        proj = dot_nt(w_in_t_ref[at : at + hidden, :], normed)
        sig = sigmoid(dot_nt(w_in_t_ref[at + hidden : at + 2 * hidden, :], normed))
        factors_ref[at : at + hidden, :] = sig
        factors_ref[at + hidden : at + 2 * hidden, :] = proj * sig * (1.0 - sig)


def contract(own_ref, other_ref, product_ref, left_ref, right_ref, own, other, natural, rows):
    core = lax.axis_index("c")
    own[...] = own_ref[...].astype(F32)
    other[...] = other_ref[...].astype(F32)
    chips = own.shape[0] // 16
    for ch in range(2):
        halves = []
        for kh in range(2):
            halves.append(
                jnp.concatenate([own[every(ch * 8 + 2 * r + kh, chips, 16), :] for r in range(2)], axis=0)
            )
            for r in range(2):
                at = every(ch * 8 + 4 + 2 * r + kh, chips, 16)
                mine, theirs = own[at, :], other[at, :]
                base = kh * 4 * chips + r
                natural[every(base, chips, 4), :] = jnp.where(core == 0, mine, theirs)
                natural[every(base + 2, chips, 4), :] = jnp.where(core == 0, theirs, mine)
        left = jnp.concatenate(halves, axis=1).astype(BF16)
        right = jnp.concatenate([natural[: 4 * chips, :], natural[4 * chips :, :]], axis=1).astype(BF16)
        left_ref[ch] = left
        right_ref[ch] = right
        product = dot_nt(left, right)
        for r in range(2):
            for jh in range(2):
                rows[every(ch * 4 + 2 * r + jh, chips, 8), :] = product[
                    r * chips : (r + 1) * chips, jh * LANES : (jh + 1) * LANES
                ]
    product_ref[...] = rows[...].astype(BF16)


def out_norm(values):
    center = values - jnp.mean(values, axis=0, keepdims=True)
    scale = lax.rsqrt(jnp.mean(center * center, axis=0, keepdims=True) + EPSILON)
    return center * scale, scale


def middle(product_ref, scaled_ref, mean_ref, grad_ref, rows, grads):
    hidden = scaled_ref.shape[0]
    rows[...] = product_ref[...].astype(F32)
    for u in range(4):
        hat, scale = out_norm(rows[every(u, hidden, 4), :])
        at = slice(u * LANES, (u + 1) * LANES)
        scaled = scaled_ref[:, at]
        both = jnp.mean(scaled * hat, axis=0, keepdims=True)
        grads[every(u, hidden, 4), :] = scale * (scaled - mean_ref[:1, at] - hat * both)
    grad_ref[...] = grads[...].astype(BF16)


def beside_middle(
    product_ref, grad_out_normed_ref, grad_lin_ref, grad_t_ref, gate_t_ref, normed_t_ref,
    w_out_ref, w_gate_ref, gain_ref, bias_ref, w_out_part_ref, w_gate_part_ref, vectors_ref, gate_term_ref,
    rows,
):
    hidden = w_out_ref.shape[0]
    rows[...] = product_ref[...].astype(F32)
    hats, normed = [], []
    gain, bias = column(gain_ref[...]), column(bias_ref[...])
    for u in range(4):
        hat, _ = out_norm(rows[every(u, hidden, 4), :])
        hats.append(hat)
        normed.append((hat * gain + bias).astype(BF16))
    hat = jnp.concatenate(hats, axis=1)
    out_normed = jnp.concatenate(normed, axis=1)
    w_out_t = jnp.transpose(w_out_ref[...].astype(F32)).astype(BF16)
    outlin = dot_nn(w_out_t, out_normed)
    gate = gate_t_ref[...]
    grad_gate = (grad_t_ref[...] * outlin * gate * (1.0 - gate)).astype(BF16)
    w_out_part_ref[...] = dot_nt(out_normed, grad_lin_ref[...])
    w_gate_part_ref[...] = dot_nt(normed_t_ref[...], grad_gate)
    gate_term_ref[...] = dot_nn(w_gate_ref[...], grad_gate)
    grad_out_normed = grad_out_normed_ref[...]
    vectors_ref[...] = columns(
        jnp.sum(grad_out_normed * hat, axis=1, keepdims=True),
        jnp.sum(grad_out_normed, axis=1, keepdims=True),
    )


def columns(*sums):
    lane = lax.broadcasted_iota(jnp.int32, (sums[0].shape[0], LANES), 1)
    high = [value.astype(BF16).astype(F32) for value in sums]
    out = jnp.zeros(lane.shape, F32)
    for n, value in enumerate(high + [value - top for value, top in zip(sums, high)]):
        out = jnp.where(lane == n, value, out)
    return out


def contract_back(grad_ref, left_ref, right_ref, grad_left_ref, keep_ref, give_ref, rows, natural):
    core = lax.axis_index("c")
    rows[...] = grad_ref[...].astype(F32)
    chips = rows.shape[0] // 8
    pieces = []
    for ch in range(2):
        halves = []
        for jh in range(2):
            halves.append(
                jnp.concatenate([rows[every(ch * 4 + 2 * r + jh, chips, 8), :] for r in range(2)], axis=0)
            )
        grad = jnp.concatenate(halves, axis=1)
        grad_t = jnp.transpose(grad).astype(BF16)
        grad_right = dot_nn(grad_t, left_ref[ch])
        natural[: 4 * chips, :] = grad_right[:, :LANES]
        natural[4 * chips :, :] = grad_right[:, LANES:]
        for r in range(2):
            for kh in range(2):
                base = kh * 4 * chips + r
                low = natural[every(base, chips, 4), :]
                high = natural[every(base + 2, chips, 4), :]
                at = every(ch * 4 + 2 * r + kh, chips, 8)
                keep_ref[at, :] = jnp.where(core == 0, low, high)
                give_ref[at, :] = jnp.where(core == 0, high, low)
        pieces.append(dot_nn(grad.astype(BF16), right_ref[ch]))
    for ch in range(2):
        for r in range(2):
            for kh in range(2):
                rows[every(ch * 4 + 2 * r + kh, chips, 8), :] = pieces[ch][
                    r * chips : (r + 1) * chips, kh * LANES : (kh + 1) * LANES
                ]
    grad_left_ref[...] = rows[...]


def join(grad_left_ref, keep_ref, got_ref, edges_ref):
    grad_left = grad_left_ref[...].reshape(-1, 8, LANES)
    grad_right = (keep_ref[...] + got_ref[...]).reshape(-1, 8, LANES)
    both = jnp.concatenate([grad_left, grad_right], axis=1)
    edges_ref[...] = both.reshape(-1, LANES).astype(BF16)


def rear(
    edges_ref, factors_ref, normed_t_ref, hat_t_ref, w_in_ref, gate_term_ref, w_out_part_ref, w_gate_part_ref,
    vectors_ref, keep_ref, give_ref, grad_normed_ref, lefts, rights, low, high,
):
    core = lax.axis_index("c")
    hidden = w_in_ref.shape[1] // 4
    edges = edges_ref[...].astype(F32).reshape(-1, 16, LANES)
    lefts[...] = edges[:, :8, :].reshape(-1, LANES)
    rights[...] = edges[:, 8:, :].reshape(-1, LANES)
    parts = []
    for u in range(4):
        at = slice(u * LANES, (u + 1) * LANES)
        left = lefts[every(u, hidden, 4), :]
        right = rights[every(u, hidden, 4), :]
        parts.append(
            jnp.concatenate(
                [
                    left * factors_ref[:hidden, at],
                    left * factors_ref[hidden : 2 * hidden, at],
                    right * factors_ref[2 * hidden : 3 * hidden, at],
                    right * factors_ref[3 * hidden :, at],
                ],
                axis=0,
            ).astype(BF16)
        )
    grad_projected = jnp.concatenate(parts, axis=1)
    w_in_part = dot_nt(normed_t_ref[...], grad_projected)
    grad_normed = dot_nn(w_in_ref[...], grad_projected) + gate_term_ref[...]
    grad_normed_ref[...] = grad_normed
    channels = w_in_part.shape[0]
    for t in range(3):
        low[every(t, channels, 4), :] = w_in_part[:, t * LANES : (t + 1) * LANES]
    low[every(3, channels, 4), :] = columns(
        jnp.sum(grad_normed * hat_t_ref[...], axis=1, keepdims=True),
        jnp.sum(grad_normed, axis=1, keepdims=True),
    )
    high[every(0, channels, 4), :] = w_in_part[:, 3 * LANES :]
    high[every(1, channels, 4), :] = w_gate_part_ref[...]
    high[every(2, channels, 4), :] = w_out_part_ref[...]
    high[every(3, channels, 4), :] = vectors_ref[...]
    keep_ref[...] = jnp.where(core == 0, low[...], high[...])
    give_ref[...] = jnp.where(core == 0, high[...], low[...])


def beside_rear(grad_normed_ref, hat_t_ref, scale_ref, gain_ref, pair_grad_ref):
    hat = hat_t_ref[...]
    scaled = grad_normed_ref[...] * column(gain_ref[...])
    grad = scale_ref[:1, :] * (
        scaled
        - jnp.mean(scaled, axis=0, keepdims=True)
        - hat * jnp.mean(scaled * hat, axis=0, keepdims=True)
    )
    pair_grad_ref[...] = jnp.transpose(grad).astype(BF16)


def split_vectors(values):
    lane = lax.broadcasted_iota(jnp.int32, values.shape, values.ndim - 1)
    row = lax.broadcasted_iota(jnp.int32, values.shape, values.ndim - 2)
    total = values + pltpu.roll(values, LANES - 2, values.ndim - 1)
    high = total.astype(BF16).astype(F32)
    low = pltpu.roll(total - high, 2, values.ndim - 1)
    return jnp.where(row % 4 == 3, jnp.where(lane < 2, high, jnp.where(lane < 4, low, 0.0)), values)


def add(keep_ref, got_ref, sum_ref):
    sum_ref[...] = split_vectors(keep_ref[...] + got_ref[...]).astype(BF16)


def reduce_share(parts_ref, share_ref):
    total = split_vectors(jnp.sum(parts_ref[...].astype(F32).reshape(-1, 8, LANES), axis=0))
    share_ref[...] = (
        jnp.broadcast_to(total[None], (share_ref.shape[0] // 8, 8, LANES))
        .reshape(share_ref.shape)
        .astype(BF16)
    )


def finish(
    own_ref, other_ref, w_in_ref, w_gate_ref, w_out_ref, in_gain_ref, in_bias_ref, out_gain_ref, out_bias_ref, low, high
):
    core = lax.axis_index("c")
    own = jnp.sum(own_ref[...].astype(F32).reshape(2, *low.shape), axis=0)
    other = jnp.sum(other_ref[...].astype(F32).reshape(2, *low.shape), axis=0)
    low[...] = jnp.where(core == 0, own, other)
    high[...] = jnp.where(core == 0, other, own)
    channels = w_in_ref.shape[0]
    for t in range(3):
        w_in_ref[:, t * LANES : (t + 1) * LANES] = low[every(t, channels, 4), :]
    w_in_ref[:, 3 * LANES :] = high[every(0, channels, 4), :]
    w_gate_ref[...] = high[every(1, channels, 4), :]
    w_out_ref[...] = high[every(2, channels, 4), :]
    inner = jnp.transpose(low[every(3, channels, 4), :])
    outer = jnp.transpose(high[every(3, channels, 4), :])
    inner, outer = inner[:2] + inner[2:4], outer[:2] + outer[2:4]
    in_gain_ref[...], in_bias_ref[...] = inner[:1], inner[1:2]
    out_gain_ref[...], out_bias_ref[...] = outer[:1], outer[1:2]


def on_device(
    pair, grad_out, w_in, w_gate, w_out, ln_in_gain, ln_in_bias, ln_out_gain, ln_out_bias
):
    shape = pair.shape
    channels = shape[3]
    hidden = w_out.shape[0]
    cells = shape[1] * shape[2]
    full_len = shape[2]
    pair2 = pair.reshape(cells, channels)
    grad2 = grad_out.reshape(cells, channels)
    in_gain_row, in_bias_row = ln_in_gain.reshape(1, -1), ln_in_bias.reshape(1, -1)
    out_gain_row, out_bias_row = ln_out_gain.reshape(1, -1), ln_out_bias.reshape(1, -1)
    grid = (hidden, cells)
    quarter = (4 * hidden, LANES)
    whole = (8 * hidden, LANES)
    to_chips = lambda a: lax.all_to_all(a, CHIPS, 0, 0, tiled=True)
    to_peers = lambda a: lax.all_to_all(a, PEERS, 0, 0, tiled=True)
    stay = lambda a: pltpu.with_memory_space_constraint(a, pltpu.HBM)
    swap = lambda a: lax.ppermute(a, "c", SWAP)

    edges, normed, w_in_t = call(
        front, [(whole, BF16), ((cells, channels), BF16), ((4 * hidden, channels), BF16)],
        [
            whole, pltpu.VMEM((cells, channels), BF16), pltpu.VMEM(w_in.shape, BF16), (1, channels), (1, channels),
            pltpu.SemaphoreType.DMA((4,)),
        ],
        far=4,
    )(stay(pair2), stay(in_gain_row), stay(in_bias_row), stay(w_in))
    own, normed = lax.optimization_barrier((to_chips(edges), normed))
    other = swap(own)
    normed_t, hat_t, scale, factors, grad_t, gate_t, grad_lin, grad_out_normed, scaled, mean = call(
        beside_front,
        [
            (grid, BF16), (grid, F32), ((8, cells), F32), ((4 * hidden, cells), F32), (grid, F32), (grid, F32),
            (grid, BF16), (grid, F32), (grid, F32), ((8, cells), F32),
        ],
        work=1 << 28,
    )(normed, pair2, grad2, w_in_t, w_gate, w_out, out_gain_row)
    other, normed_t = lax.optimization_barrier((other, normed_t))
    product, left, right = call(
        contract,
        [(quarter, BF16), ((2, full_len // 2, full_len), BF16), ((2, full_len, full_len), BF16)],
        [whole, whole, quarter, quarter],
    )(own, other)
    product = to_chips(product)
    (grad_product,) = call(middle, [(quarter, BF16)], [quarter, quarter])(product, scaled, mean)
    grad_cols = to_chips(grad_product)
    grad_left, keep, give = call(contract_back, [(quarter, F32)] * 3, [quarter, quarter])(
        grad_cols, left, right
    )
    give, product = lax.optimization_barrier((give, product))
    got = swap(give)
    w_out_part, w_gate_part, vectors, gate_term = call(
        beside_middle,
        [((hidden, channels), F32), ((channels, channels), F32), ((hidden, LANES), F32), (grid, F32)],
        [quarter],
        work=1 << 28,
    )(product, grad_out_normed, grad_lin, grad_t, gate_t, normed_t, w_out, w_gate, out_gain_row, out_bias_row)
    got, vectors = lax.optimization_barrier((got, vectors))
    (grad_edges,) = call(join, [(whole, BF16)])(grad_left, keep, got)
    grad_edges = to_chips(grad_edges)
    keep, give, grad_normed = call(
        rear, [(quarter, F32), (quarter, F32), (grid, F32)], [quarter] * 4
    )(grad_edges, factors, normed_t, hat_t, w_in, gate_term, w_out_part, w_gate_part, vectors)
    got = swap(give)
    (pair_grad,) = call(beside_rear, [((cells, channels), BF16)], work=1 << 28)(
        grad_normed, hat_t, scale, in_gain_row
    )
    got, pair_grad = lax.optimization_barrier((got, pair_grad))
    (parts,) = call(add, [(quarter, BF16)])(keep, got)
    (share,) = call(reduce_share, [(whole, BF16)])(to_chips(parts))
    mine = to_peers(share)
    w_in_total, w_gate_total, w_out_total, *vectors = call(
        finish,
        [(w_in.shape, F32), (w_gate.shape, F32), (w_out.shape, F32)] + [((1, LANES), F32)] * 4,
        [quarter, quarter],
    )(mine, swap(mine))
    return (
        pair_grad.reshape(shape),
        w_in_total,
        w_gate_total,
        w_out_total,
        *(vector.reshape(-1) for vector in vectors),
    )


def solution(mesh):
    fine = Mesh(mesh.devices.reshape(2, 2, 8, 4, 2), ("X", "x", "z", "y", "c"))
    cells = P("X", ("x", "z", "y", "c"), None, None)
    in_specs = (cells, cells, P(), P(), P(), P(), P(), P(), P())
    out_specs = (cells, P(), P(), P(), P(), P(), P(), P())
    return jax.shard_map(
        on_device, mesh=fine, in_specs=in_specs, out_specs=out_specs, check_vma=False
    )
```

```python
import functools

import jax
import jax.numpy as jnp
from jax import lax
from jax.experimental import pallas as pl
from jax.experimental.pallas import tpu as pltpu
from jax.sharding import Mesh, PartitionSpec as P

EPSILON = 1e-05
CHIPS = ("x", "z", "y")
SWAP = [(0, 1), (1, 0)]
LANES = 128
F32 = jnp.float32
BF16 = jnp.bfloat16


def call(body, outs, scratch=(), work=0, far=0):
    def run(*operands):
        return pl.pallas_call(
            body,
            out_shape=[jax.ShapeDtypeStruct(shape, dtype) for shape, dtype in outs],
            in_specs=[pl.BlockSpec(memory_space=pltpu.HBM)] * far
            + [pl.BlockSpec(memory_space=pltpu.VMEM)] * (len(operands) - far),
            out_specs=[pl.BlockSpec(memory_space=pltpu.VMEM)] * len(outs),
            scratch_shapes=[pltpu.VMEM(s, F32) if isinstance(s, tuple) else s for s in scratch],
            compiler_params=pltpu.CompilerParams(vmem_limit_bytes=8 * 1024 * 1024),
            cost_estimate=pl.CostEstimate(
                flops=work, bytes_accessed=1 << 20, transcendentals=0
            ),
        )(*operands)

    return run


def dot_nt(a, b):
    return lax.dot_general(a, b, (((1,), (1,)), ((), ())), preferred_element_type=F32)


def dot_nn(a, b):
    return lax.dot_general(a, b, (((1,), (0,)), ((), ())), preferred_element_type=F32)


def sigmoid(x):
    return jax.nn.sigmoid(x)


def every(start, count, stride):
    return pl.ds(start, count, stride=stride)


def column(row):
    return jnp.transpose(jnp.broadcast_to(row, (LANES, row.shape[1])))[:, :1]


def front(
    pair_far, gain_far, bias_far, w_in_far, edges_ref, normed_ref, w_in_t_ref,
    rows, pair_ref, w_in_ref, gain_ref, bias_ref, arrived,
):
    copies = [
        pltpu.make_async_copy(source, target, arrived.at[n])
        for n, (source, target) in enumerate(
            [(pair_far, pair_ref), (gain_far, gain_ref), (bias_far, bias_ref), (w_in_far, w_in_ref)]
        )
    ]
    for copy in copies:
        copy.start()
    for copy in copies[:3]:
        copy.wait()
    values = pair_ref[...].astype(F32)
    center = values - jnp.mean(values, axis=1, keepdims=True)
    scale = lax.rsqrt(jnp.mean(center * center, axis=1, keepdims=True) + EPSILON)
    normed = (center * scale * gain_ref[...] + bias_ref[...]).astype(BF16)
    normed_ref[...] = normed
    copies[3].wait()
    w_in_t = jnp.transpose(w_in_ref[...].astype(F32)).astype(BF16)
    w_in_t_ref[...] = w_in_t
    hidden = w_in_t.shape[0] // 4
    for side in range(2):
        proj = dot_nt(w_in_t[2 * side * hidden : (2 * side + 1) * hidden], normed)
        gate = dot_nt(w_in_t[(2 * side + 1) * hidden : (2 * side + 2) * hidden], normed)
        value = sigmoid(gate) * proj
        for u in range(4):
            rows[every(4 * side + u, hidden, 8), :] = value[:, u * LANES : (u + 1) * LANES]
    edges_ref[...] = rows[...].astype(BF16)


def beside_front(
    normed_ref, pair_ref, grad_ref, w_in_t_ref, w_gate_ref, w_out_ref, gain_ref,
    normed_t_ref, hat_t_ref, scale_ref, factors_ref, grad_t_ref, gate_t_ref, grad_lin_ref,
    grad_out_normed_ref, scaled_ref, mean_ref,
):
    hidden = w_out_ref.shape[0]
    normed = normed_ref[...]
    normed_t_ref[...] = jnp.transpose(normed.astype(F32)).astype(BF16)
    values = jnp.transpose(pair_ref[...].astype(F32))
    center = values - jnp.mean(values, axis=0, keepdims=True)
    scale = lax.rsqrt(jnp.mean(center * center, axis=0, keepdims=True) + EPSILON)
    hat_t_ref[...] = center * scale
    scale_ref[...] = jnp.broadcast_to(scale, scale_ref.shape)
    grad_t = jnp.transpose(grad_ref[...].astype(F32))
    grad_t_ref[...] = grad_t
    w_gate_t = jnp.transpose(w_gate_ref[...].astype(F32)).astype(BF16)
    gate = sigmoid(dot_nt(w_gate_t, normed))
    gate_t_ref[...] = gate
    grad_lin = (grad_t * gate).astype(BF16)
    grad_lin_ref[...] = grad_lin
    grad_out_normed = dot_nn(w_out_ref[...], grad_lin)
    grad_out_normed_ref[...] = grad_out_normed
    scaled = grad_out_normed * column(gain_ref[...])
    scaled_ref[...] = scaled
    mean_ref[...] = jnp.broadcast_to(jnp.mean(scaled, axis=0, keepdims=True), mean_ref.shape)
    for side in range(2):
        at = 2 * side * hidden
        proj = dot_nt(w_in_t_ref[at : at + hidden, :], normed)
        sig = sigmoid(dot_nt(w_in_t_ref[at + hidden : at + 2 * hidden, :], normed))
        factors_ref[at : at + hidden, :] = sig
        factors_ref[at + hidden : at + 2 * hidden, :] = proj * sig * (1.0 - sig)


def contract(own_ref, other_ref, product_ref, left_ref, right_ref, own, other, natural, rows):
    core = lax.axis_index("c")
    own[...] = own_ref[...].astype(F32)
    other[...] = other_ref[...].astype(F32)
    chips = own.shape[0] // 16
    for ch in range(2):
        halves = []
        for kh in range(2):
            halves.append(
                jnp.concatenate([own[every(ch * 8 + 2 * r + kh, chips, 16), :] for r in range(2)], axis=0)
            )
            for r in range(2):
                at = every(ch * 8 + 4 + 2 * r + kh, chips, 16)
                mine, theirs = own[at, :], other[at, :]
                base = kh * 4 * chips + r
                natural[every(base, chips, 4), :] = jnp.where(core == 0, mine, theirs)
                natural[every(base + 2, chips, 4), :] = jnp.where(core == 0, theirs, mine)
        left = jnp.concatenate(halves, axis=1).astype(BF16)
        right = jnp.concatenate([natural[: 4 * chips, :], natural[4 * chips :, :]], axis=1).astype(BF16)
        left_ref[ch] = left
        right_ref[ch] = right
        product = dot_nt(left, right)
        for r in range(2):
            for jh in range(2):
                rows[every(ch * 4 + 2 * r + jh, chips, 8), :] = product[
                    r * chips : (r + 1) * chips, jh * LANES : (jh + 1) * LANES
                ]
    product_ref[...] = rows[...].astype(BF16)


def out_norm(values):
    center = values - jnp.mean(values, axis=0, keepdims=True)
    scale = lax.rsqrt(jnp.mean(center * center, axis=0, keepdims=True) + EPSILON)
    return center * scale, scale


def middle(product_ref, scaled_ref, mean_ref, grad_ref, rows, grads):
    hidden = scaled_ref.shape[0]
    rows[...] = product_ref[...].astype(F32)
    for u in range(4):
        hat, scale = out_norm(rows[every(u, hidden, 4), :])
        at = slice(u * LANES, (u + 1) * LANES)
        scaled = scaled_ref[:, at]
        both = jnp.mean(scaled * hat, axis=0, keepdims=True)
        grads[every(u, hidden, 4), :] = scale * (scaled - mean_ref[:1, at] - hat * both)
    grad_ref[...] = grads[...].astype(BF16)


def beside_middle(
    product_ref, grad_out_normed_ref, grad_lin_ref, grad_t_ref, gate_t_ref, normed_t_ref,
    w_out_ref, w_gate_ref, gain_ref, bias_ref, w_out_part_ref, w_gate_part_ref, vectors_ref, gate_term_ref,
    rows,
):
    hidden = w_out_ref.shape[0]
    rows[...] = product_ref[...].astype(F32)
    hats, normed = [], []
    gain, bias = column(gain_ref[...]), column(bias_ref[...])
    for u in range(4):
        hat, _ = out_norm(rows[every(u, hidden, 4), :])
        hats.append(hat)
        normed.append((hat * gain + bias).astype(BF16))
    hat = jnp.concatenate(hats, axis=1)
    out_normed = jnp.concatenate(normed, axis=1)
    w_out_t = jnp.transpose(w_out_ref[...].astype(F32)).astype(BF16)
    outlin = dot_nn(w_out_t, out_normed)
    gate = gate_t_ref[...]
    grad_gate = (grad_t_ref[...] * outlin * gate * (1.0 - gate)).astype(BF16)
    w_out_part_ref[...] = dot_nt(out_normed, grad_lin_ref[...])
    w_gate_part_ref[...] = dot_nt(normed_t_ref[...], grad_gate)
    gate_term_ref[...] = dot_nn(w_gate_ref[...], grad_gate)
    grad_out_normed = grad_out_normed_ref[...]
    vectors_ref[...] = columns(
        jnp.sum(grad_out_normed * hat, axis=1, keepdims=True),
        jnp.sum(grad_out_normed, axis=1, keepdims=True),
    )


def columns(*sums):
    lane = lax.broadcasted_iota(jnp.int32, (sums[0].shape[0], LANES), 1)
    high = [value.astype(BF16).astype(F32) for value in sums]
    out = jnp.zeros(lane.shape, F32)
    for n, value in enumerate(high + [value - top for value, top in zip(sums, high)]):
        out = jnp.where(lane == n, value, out)
    return out


def contract_back(grad_ref, left_ref, right_ref, grad_left_ref, keep_ref, give_ref, rows, natural):
    core = lax.axis_index("c")
    rows[...] = grad_ref[...].astype(F32)
    chips = rows.shape[0] // 8
    pieces = []
    for ch in range(2):
        halves = []
        for jh in range(2):
            halves.append(
                jnp.concatenate([rows[every(ch * 4 + 2 * r + jh, chips, 8), :] for r in range(2)], axis=0)
            )
        grad = jnp.concatenate(halves, axis=1)
        grad_t = jnp.transpose(grad).astype(BF16)
        grad_right = dot_nn(grad_t, left_ref[ch])
        natural[: 4 * chips, :] = grad_right[:, :LANES]
        natural[4 * chips :, :] = grad_right[:, LANES:]
        for r in range(2):
            for kh in range(2):
                base = kh * 4 * chips + r
                low = natural[every(base, chips, 4), :]
                high = natural[every(base + 2, chips, 4), :]
                at = every(ch * 4 + 2 * r + kh, chips, 8)
                keep_ref[at, :] = jnp.where(core == 0, low, high)
                give_ref[at, :] = jnp.where(core == 0, high, low)
        pieces.append(dot_nn(grad.astype(BF16), right_ref[ch]))
    for ch in range(2):
        for r in range(2):
            for kh in range(2):
                rows[every(ch * 4 + 2 * r + kh, chips, 8), :] = pieces[ch][
                    r * chips : (r + 1) * chips, kh * LANES : (kh + 1) * LANES
                ]
    grad_left_ref[...] = rows[...]


def join(grad_left_ref, keep_ref, got_ref, edges_ref):
    grad_left = grad_left_ref[...].reshape(-1, 8, LANES)
    grad_right = (keep_ref[...] + got_ref[...]).reshape(-1, 8, LANES)
    both = jnp.concatenate([grad_left, grad_right], axis=1)
    edges_ref[...] = both.reshape(-1, LANES).astype(BF16)


def rear(
    edges_ref, factors_ref, normed_t_ref, hat_t_ref, w_in_ref, gate_term_ref, w_out_part_ref, w_gate_part_ref,
    vectors_ref, keep_ref, give_ref, grad_normed_ref, lefts, rights, low, high,
):
    core = lax.axis_index("c")
    hidden = w_in_ref.shape[1] // 4
    edges = edges_ref[...].astype(F32).reshape(-1, 16, LANES)
    lefts[...] = edges[:, :8, :].reshape(-1, LANES)
    rights[...] = edges[:, 8:, :].reshape(-1, LANES)
    parts = []
    for u in range(4):
        at = slice(u * LANES, (u + 1) * LANES)
        left = lefts[every(u, hidden, 4), :]
        right = rights[every(u, hidden, 4), :]
        parts.append(
            jnp.concatenate(
                [
                    left * factors_ref[:hidden, at],
                    left * factors_ref[hidden : 2 * hidden, at],
                    right * factors_ref[2 * hidden : 3 * hidden, at],
                    right * factors_ref[3 * hidden :, at],
                ],
                axis=0,
            ).astype(BF16)
        )
    grad_projected = jnp.concatenate(parts, axis=1)
    w_in_part = dot_nt(normed_t_ref[...], grad_projected)
    grad_normed = dot_nn(w_in_ref[...], grad_projected) + gate_term_ref[...]
    grad_normed_ref[...] = grad_normed
    channels = w_in_part.shape[0]
    for t in range(3):
        low[every(t, channels, 4), :] = w_in_part[:, t * LANES : (t + 1) * LANES]
    low[every(3, channels, 4), :] = columns(
        jnp.sum(grad_normed * hat_t_ref[...], axis=1, keepdims=True),
        jnp.sum(grad_normed, axis=1, keepdims=True),
    )
    high[every(0, channels, 4), :] = w_in_part[:, 3 * LANES :]
    high[every(1, channels, 4), :] = w_gate_part_ref[...]
    high[every(2, channels, 4), :] = w_out_part_ref[...]
    high[every(3, channels, 4), :] = vectors_ref[...]
    keep_ref[...] = jnp.where(core == 0, low[...], high[...])
    give_ref[...] = jnp.where(core == 0, high[...], low[...])


def beside_rear(grad_normed_ref, hat_t_ref, scale_ref, gain_ref, pair_grad_ref):
    hat = hat_t_ref[...]
    scaled = grad_normed_ref[...] * column(gain_ref[...])
    grad = scale_ref[:1, :] * (
        scaled
        - jnp.mean(scaled, axis=0, keepdims=True)
        - hat * jnp.mean(scaled * hat, axis=0, keepdims=True)
    )
    pair_grad_ref[...] = jnp.transpose(grad).astype(BF16)


def split_vectors(values):
    lane = lax.broadcasted_iota(jnp.int32, values.shape, values.ndim - 1)
    row = lax.broadcasted_iota(jnp.int32, values.shape, values.ndim - 2)
    total = values + pltpu.roll(values, LANES - 2, values.ndim - 1)
    high = total.astype(BF16).astype(F32)
    low = pltpu.roll(total - high, 2, values.ndim - 1)
    return jnp.where(row % 4 == 3, jnp.where(lane < 2, high, jnp.where(lane < 4, low, 0.0)), values)


def add(keep_ref, got_ref, sum_ref):
    sum_ref[...] = split_vectors(keep_ref[...] + got_ref[...]).astype(BF16)


def reduce_share(parts_ref, share_ref):
    share_ref[...] = jnp.sum(parts_ref[...].astype(F32).reshape(-1, 8, LANES), axis=0)


def spread(share_ref, got_ref, copies_ref):
    total = split_vectors(share_ref[...] + got_ref[...])
    copies_ref[...] = (
        jnp.broadcast_to(total[None], (copies_ref.shape[0] // 8, 8, LANES))
        .reshape(copies_ref.shape)
        .astype(BF16)
    )


def finish(
    own_ref, other_ref, w_in_ref, w_gate_ref, w_out_ref, in_gain_ref, in_bias_ref, out_gain_ref, out_bias_ref, low, high
):
    core = lax.axis_index("c")
    own, other = own_ref[...].astype(F32), other_ref[...].astype(F32)
    low[...] = jnp.where(core == 0, own, other)
    high[...] = jnp.where(core == 0, other, own)
    channels = w_in_ref.shape[0]
    for t in range(3):
        w_in_ref[:, t * LANES : (t + 1) * LANES] = low[every(t, channels, 4), :]
    w_in_ref[:, 3 * LANES :] = high[every(0, channels, 4), :]
    w_gate_ref[...] = high[every(1, channels, 4), :]
    w_out_ref[...] = high[every(2, channels, 4), :]
    inner = jnp.transpose(low[every(3, channels, 4), :])
    outer = jnp.transpose(high[every(3, channels, 4), :])
    inner, outer = inner[:2] + inner[2:4], outer[:2] + outer[2:4]
    in_gain_ref[...], in_bias_ref[...] = inner[:1], inner[1:2]
    out_gain_ref[...], out_bias_ref[...] = outer[:1], outer[1:2]


def on_device(
    pair, grad_out, w_in, w_gate, w_out, ln_in_gain, ln_in_bias, ln_out_gain, ln_out_bias
):
    shape = pair.shape
    channels = shape[3]
    hidden = w_out.shape[0]
    cells = shape[1] * shape[2]
    full_len = shape[2]
    pair2 = pair.reshape(cells, channels)
    grad2 = grad_out.reshape(cells, channels)
    in_gain_row, in_bias_row = ln_in_gain.reshape(1, -1), ln_in_bias.reshape(1, -1)
    out_gain_row, out_bias_row = ln_out_gain.reshape(1, -1), ln_out_bias.reshape(1, -1)
    grid = (hidden, cells)
    quarter = (4 * hidden, LANES)
    whole = (8 * hidden, LANES)
    to_chips = lambda a: lax.all_to_all(a, CHIPS, 0, 0, tiled=True)
    stay = lambda a: pltpu.with_memory_space_constraint(a, pltpu.HBM)
    swap = lambda a: lax.ppermute(a, "c", SWAP)

    edges, normed, w_in_t = call(
        front, [(whole, BF16), ((cells, channels), BF16), ((4 * hidden, channels), BF16)],
        [
            whole, pltpu.VMEM((cells, channels), BF16), pltpu.VMEM(w_in.shape, BF16), (1, channels), (1, channels),
            pltpu.SemaphoreType.DMA((4,)),
        ],
        far=4,
    )(stay(pair2), stay(in_gain_row), stay(in_bias_row), stay(w_in))
    own, normed = lax.optimization_barrier((to_chips(edges), normed))
    other = swap(own)
    normed_t, hat_t, scale, factors, grad_t, gate_t, grad_lin, grad_out_normed, scaled, mean = call(
        beside_front,
        [
            (grid, BF16), (grid, F32), ((8, cells), F32), ((4 * hidden, cells), F32), (grid, F32), (grid, F32),
            (grid, BF16), (grid, F32), (grid, F32), ((8, cells), F32),
        ],
        work=1 << 28,
    )(normed, pair2, grad2, w_in_t, w_gate, w_out, out_gain_row)
    other, normed_t = lax.optimization_barrier((other, normed_t))
    product, left, right = call(
        contract,
        [(quarter, BF16), ((2, full_len // 2, full_len), BF16), ((2, full_len, full_len), BF16)],
        [whole, whole, quarter, quarter],
    )(own, other)
    product = to_chips(product)
    (grad_product,) = call(middle, [(quarter, BF16)], [quarter, quarter])(product, scaled, mean)
    grad_cols = to_chips(grad_product)
    grad_left, keep, give = call(contract_back, [(quarter, F32)] * 3, [quarter, quarter])(
        grad_cols, left, right
    )
    give, product = lax.optimization_barrier((give, product))
    got = swap(give)
    w_out_part, w_gate_part, vectors, gate_term = call(
        beside_middle,
        [((hidden, channels), F32), ((channels, channels), F32), ((hidden, LANES), F32), (grid, F32)],
        [quarter],
        work=1 << 28,
    )(product, grad_out_normed, grad_lin, grad_t, gate_t, normed_t, w_out, w_gate, out_gain_row, out_bias_row)
    got, vectors = lax.optimization_barrier((got, vectors))
    (grad_edges,) = call(join, [(whole, BF16)])(grad_left, keep, got)
    grad_edges = to_chips(grad_edges)
    keep, give, grad_normed = call(
        rear, [(quarter, F32), (quarter, F32), (grid, F32)], [quarter] * 4
    )(grad_edges, factors, normed_t, hat_t, w_in, gate_term, w_out_part, w_gate_part, vectors)
    got = swap(give)
    (pair_grad,) = call(beside_rear, [((cells, channels), BF16)], work=1 << 28)(
        grad_normed, hat_t, scale, in_gain_row
    )
    got, pair_grad = lax.optimization_barrier((got, pair_grad))
    (parts,) = call(add, [(quarter, BF16)])(keep, got)
    (share,) = call(reduce_share, [((8, LANES), F32)])(to_chips(parts))
    (copies,) = call(spread, [(quarter, BF16)])(share, lax.ppermute(share, "X", SWAP))
    mine = to_chips(copies)
    w_in_total, w_gate_total, w_out_total, *vectors = call(
        finish,
        [(w_in.shape, F32), (w_gate.shape, F32), (w_out.shape, F32)] + [((1, LANES), F32)] * 4,
        [quarter, quarter],
    )(mine, swap(mine))
    return (
        pair_grad.reshape(shape),
        w_in_total,
        w_gate_total,
        w_out_total,
        *(vector.reshape(-1) for vector in vectors),
    )


def solution(mesh):
    fine = Mesh(mesh.devices.reshape(2, 2, 8, 4, 2), ("X", "x", "z", "y", "c"))
    cells = P("X", ("x", "z", "y", "c"), None, None)
    in_specs = (cells, cells, P(), P(), P(), P(), P(), P(), P())
    out_specs = (cells, P(), P(), P(), P(), P(), P(), P())
    return jax.shard_map(
        on_device, mesh=fine, in_specs=in_specs, out_specs=out_specs, check_vma=False
    )
```

```python
import functools

import jax
import jax.numpy as jnp
from jax import lax
from jax.experimental import pallas as pl
from jax.experimental.pallas import tpu as pltpu
from jax.sharding import Mesh, PartitionSpec as P

EPSILON = 1e-05
CHIPS = ("x", "z", "y")
SWAP = [(0, 1), (1, 0)]
LANES = 128
F32 = jnp.float32
BF16 = jnp.bfloat16


def call(body, outs, scratch=(), work=0, far=0):
    def run(*operands):
        return pl.pallas_call(
            body,
            out_shape=[jax.ShapeDtypeStruct(shape, dtype) for shape, dtype in outs],
            in_specs=[pl.BlockSpec(memory_space=pltpu.HBM)] * far
            + [pl.BlockSpec(memory_space=pltpu.VMEM)] * (len(operands) - far),
            out_specs=[pl.BlockSpec(memory_space=pltpu.VMEM)] * len(outs),
            scratch_shapes=[pltpu.VMEM(s, F32) if isinstance(s, tuple) else s for s in scratch],
            compiler_params=pltpu.CompilerParams(vmem_limit_bytes=8 * 1024 * 1024),
            cost_estimate=pl.CostEstimate(
                flops=work, bytes_accessed=1 << 20, transcendentals=0
            ),
        )(*operands)

    return run


def dot_nt(a, b):
    return lax.dot_general(a, b, (((1,), (1,)), ((), ())), preferred_element_type=F32)


def dot_nn(a, b):
    return lax.dot_general(a, b, (((1,), (0,)), ((), ())), preferred_element_type=F32)


def sigmoid(x):
    return jax.nn.sigmoid(x)


def first_half():
    return lax.axis_index("c") == lax.axis_index("X")


def every(start, count, stride):
    return pl.ds(start, count, stride=stride)


def column(row):
    return jnp.transpose(jnp.broadcast_to(row, (LANES, row.shape[1])))[:, :1]


def front(
    pair_far, gain_far, bias_far, w_in_far, edges_ref, normed_ref, w_in_t_ref,
    rows, pair_ref, w_in_ref, gain_ref, bias_ref, arrived,
):
    copies = [
        pltpu.make_async_copy(source, target, arrived.at[n])
        for n, (source, target) in enumerate(
            [(pair_far, pair_ref), (gain_far, gain_ref), (bias_far, bias_ref), (w_in_far, w_in_ref)]
        )
    ]
    for copy in copies:
        copy.start()
    for copy in copies[:3]:
        copy.wait()
    values = pair_ref[...].astype(F32)
    center = values - jnp.mean(values, axis=1, keepdims=True)
    scale = lax.rsqrt(jnp.mean(center * center, axis=1, keepdims=True) + EPSILON)
    normed = (center * scale * gain_ref[...] + bias_ref[...]).astype(BF16)
    normed_ref[...] = normed
    copies[3].wait()
    w_in_t = jnp.transpose(w_in_ref[...].astype(F32)).astype(BF16)
    w_in_t_ref[...] = w_in_t
    hidden = w_in_t.shape[0] // 4
    for side in range(2):
        proj = dot_nt(w_in_t[2 * side * hidden : (2 * side + 1) * hidden], normed)
        gate = dot_nt(w_in_t[(2 * side + 1) * hidden : (2 * side + 2) * hidden], normed)
        value = sigmoid(gate) * proj
        for u in range(4):
            rows[every(4 * side + u, hidden, 8), :] = value[:, u * LANES : (u + 1) * LANES]
    edges_ref[...] = rows[...].astype(BF16)


def beside_front(
    normed_ref, pair_ref, grad_ref, w_in_t_ref, w_gate_ref, w_out_ref, gain_ref,
    normed_t_ref, hat_t_ref, scale_ref, factors_ref, grad_t_ref, gate_t_ref, grad_lin_ref,
    grad_out_normed_ref, scaled_ref, mean_ref,
):
    hidden = w_out_ref.shape[0]
    normed = normed_ref[...]
    normed_t_ref[...] = jnp.transpose(normed.astype(F32)).astype(BF16)
    values = jnp.transpose(pair_ref[...].astype(F32))
    center = values - jnp.mean(values, axis=0, keepdims=True)
    scale = lax.rsqrt(jnp.mean(center * center, axis=0, keepdims=True) + EPSILON)
    hat_t_ref[...] = center * scale
    scale_ref[...] = jnp.broadcast_to(scale, scale_ref.shape)
    grad_t = jnp.transpose(grad_ref[...].astype(F32))
    grad_t_ref[...] = grad_t
    w_gate_t = jnp.transpose(w_gate_ref[...].astype(F32)).astype(BF16)
    gate = sigmoid(dot_nt(w_gate_t, normed))
    gate_t_ref[...] = gate
    grad_lin = (grad_t * gate).astype(BF16)
    grad_lin_ref[...] = grad_lin
    grad_out_normed = dot_nn(w_out_ref[...], grad_lin)
    grad_out_normed_ref[...] = grad_out_normed
    scaled = grad_out_normed * column(gain_ref[...])
    scaled_ref[...] = scaled
    mean_ref[...] = jnp.broadcast_to(jnp.mean(scaled, axis=0, keepdims=True), mean_ref.shape)
    for side in range(2):
        at = 2 * side * hidden
        proj = dot_nt(w_in_t_ref[at : at + hidden, :], normed)
        sig = sigmoid(dot_nt(w_in_t_ref[at + hidden : at + 2 * hidden, :], normed))
        factors_ref[at : at + hidden, :] = sig
        factors_ref[at + hidden : at + 2 * hidden, :] = proj * sig * (1.0 - sig)


def contract(own_ref, other_ref, product_ref, left_ref, right_ref, own, other, natural, rows):
    core = lax.axis_index("c")
    own[...] = own_ref[...].astype(F32)
    other[...] = other_ref[...].astype(F32)
    chips = own.shape[0] // 16
    for ch in range(2):
        halves = []
        for kh in range(2):
            halves.append(
                jnp.concatenate([own[every(ch * 8 + 2 * r + kh, chips, 16), :] for r in range(2)], axis=0)
            )
            for r in range(2):
                at = every(ch * 8 + 4 + 2 * r + kh, chips, 16)
                mine, theirs = own[at, :], other[at, :]
                base = kh * 4 * chips + r
                natural[every(base, chips, 4), :] = jnp.where(core == 0, mine, theirs)
                natural[every(base + 2, chips, 4), :] = jnp.where(core == 0, theirs, mine)
        left = jnp.concatenate(halves, axis=1).astype(BF16)
        right = jnp.concatenate([natural[: 4 * chips, :], natural[4 * chips :, :]], axis=1).astype(BF16)
        left_ref[ch] = left
        right_ref[ch] = right
        product = dot_nt(left, right)
        for r in range(2):
            for jh in range(2):
                rows[every(ch * 4 + 2 * r + jh, chips, 8), :] = product[
                    r * chips : (r + 1) * chips, jh * LANES : (jh + 1) * LANES
                ]
    product_ref[...] = rows[...].astype(BF16)


def out_norm(values):
    center = values - jnp.mean(values, axis=0, keepdims=True)
    scale = lax.rsqrt(jnp.mean(center * center, axis=0, keepdims=True) + EPSILON)
    return center * scale, scale


def middle(product_ref, scaled_ref, mean_ref, grad_ref, rows, grads):
    hidden = scaled_ref.shape[0]
    rows[...] = product_ref[...].astype(F32)
    for u in range(4):
        hat, scale = out_norm(rows[every(u, hidden, 4), :])
        at = slice(u * LANES, (u + 1) * LANES)
        scaled = scaled_ref[:, at]
        both = jnp.mean(scaled * hat, axis=0, keepdims=True)
        grads[every(u, hidden, 4), :] = scale * (scaled - mean_ref[:1, at] - hat * both)
    grad_ref[...] = grads[...].astype(BF16)


def beside_middle(
    product_ref, grad_out_normed_ref, grad_lin_ref, grad_t_ref, gate_t_ref, normed_t_ref,
    w_out_ref, w_gate_ref, gain_ref, bias_ref, w_out_part_ref, w_gate_part_ref, vectors_ref, gate_term_ref,
    rows,
):
    hidden = w_out_ref.shape[0]
    rows[...] = product_ref[...].astype(F32)
    hats, normed = [], []
    gain, bias = column(gain_ref[...]), column(bias_ref[...])
    for u in range(4):
        hat, _ = out_norm(rows[every(u, hidden, 4), :])
        hats.append(hat)
        normed.append((hat * gain + bias).astype(BF16))
    hat = jnp.concatenate(hats, axis=1)
    out_normed = jnp.concatenate(normed, axis=1)
    w_out_t = jnp.transpose(w_out_ref[...].astype(F32)).astype(BF16)
    outlin = dot_nn(w_out_t, out_normed)
    gate = gate_t_ref[...]
    grad_gate = (grad_t_ref[...] * outlin * gate * (1.0 - gate)).astype(BF16)
    w_out_part_ref[...] = dot_nt(out_normed, grad_lin_ref[...])
    w_gate_part_ref[...] = dot_nt(normed_t_ref[...], grad_gate)
    gate_term_ref[...] = dot_nn(w_gate_ref[...], grad_gate)
    grad_out_normed = grad_out_normed_ref[...]
    vectors_ref[...] = columns(
        jnp.sum(grad_out_normed * hat, axis=1, keepdims=True),
        jnp.sum(grad_out_normed, axis=1, keepdims=True),
    )


def columns(*sums):
    lane = lax.broadcasted_iota(jnp.int32, (sums[0].shape[0], LANES), 1)
    high = [value.astype(BF16).astype(F32) for value in sums]
    out = jnp.zeros(lane.shape, F32)
    for n, value in enumerate(high + [value - top for value, top in zip(sums, high)]):
        out = jnp.where(lane == n, value, out)
    return out


def contract_back(grad_ref, left_ref, right_ref, grad_left_ref, keep_ref, give_ref, rows, natural):
    core = lax.axis_index("c")
    rows[...] = grad_ref[...].astype(F32)
    chips = rows.shape[0] // 8
    pieces = []
    for ch in range(2):
        halves = []
        for jh in range(2):
            halves.append(
                jnp.concatenate([rows[every(ch * 4 + 2 * r + jh, chips, 8), :] for r in range(2)], axis=0)
            )
        grad = jnp.concatenate(halves, axis=1)
        grad_t = jnp.transpose(grad).astype(BF16)
        grad_right = dot_nn(grad_t, left_ref[ch])
        natural[: 4 * chips, :] = grad_right[:, :LANES]
        natural[4 * chips :, :] = grad_right[:, LANES:]
        for r in range(2):
            for kh in range(2):
                base = kh * 4 * chips + r
                low = natural[every(base, chips, 4), :]
                high = natural[every(base + 2, chips, 4), :]
                at = every(ch * 4 + 2 * r + kh, chips, 8)
                keep_ref[at, :] = jnp.where(core == 0, low, high)
                give_ref[at, :] = jnp.where(core == 0, high, low)
        pieces.append(dot_nn(grad.astype(BF16), right_ref[ch]))
    for ch in range(2):
        for r in range(2):
            for kh in range(2):
                rows[every(ch * 4 + 2 * r + kh, chips, 8), :] = pieces[ch][
                    r * chips : (r + 1) * chips, kh * LANES : (kh + 1) * LANES
                ]
    grad_left_ref[...] = rows[...]


def join(grad_left_ref, keep_ref, got_ref, edges_ref):
    grad_left = grad_left_ref[...].reshape(-1, 8, LANES)
    grad_right = (keep_ref[...] + got_ref[...]).reshape(-1, 8, LANES)
    both = jnp.concatenate([grad_left, grad_right], axis=1)
    edges_ref[...] = both.reshape(-1, LANES).astype(BF16)


def rear(
    edges_ref, factors_ref, normed_t_ref, hat_t_ref, w_in_ref, gate_term_ref, w_out_part_ref, w_gate_part_ref,
    vectors_ref, keep_ref, give_ref, grad_normed_ref, lefts, rights, low, high,
):
    first = first_half()
    hidden = w_in_ref.shape[1] // 4
    edges = edges_ref[...].astype(F32).reshape(-1, 16, LANES)
    lefts[...] = edges[:, :8, :].reshape(-1, LANES)
    rights[...] = edges[:, 8:, :].reshape(-1, LANES)
    parts = []
    for u in range(4):
        at = slice(u * LANES, (u + 1) * LANES)
        left = lefts[every(u, hidden, 4), :]
        right = rights[every(u, hidden, 4), :]
        parts.append(
            jnp.concatenate(
                [
                    left * factors_ref[:hidden, at],
                    left * factors_ref[hidden : 2 * hidden, at],
                    right * factors_ref[2 * hidden : 3 * hidden, at],
                    right * factors_ref[3 * hidden :, at],
                ],
                axis=0,
            ).astype(BF16)
        )
    grad_projected = jnp.concatenate(parts, axis=1)
    w_in_part = dot_nt(normed_t_ref[...], grad_projected)
    grad_normed = dot_nn(w_in_ref[...], grad_projected) + gate_term_ref[...]
    grad_normed_ref[...] = grad_normed
    channels = w_in_part.shape[0]
    for t in range(3):
        low[every(t, channels, 4), :] = w_in_part[:, t * LANES : (t + 1) * LANES]
    low[every(3, channels, 4), :] = columns(
        jnp.sum(grad_normed * hat_t_ref[...], axis=1, keepdims=True),
        jnp.sum(grad_normed, axis=1, keepdims=True),
    )
    high[every(0, channels, 4), :] = w_in_part[:, 3 * LANES :]
    high[every(1, channels, 4), :] = w_gate_part_ref[...]
    high[every(2, channels, 4), :] = w_out_part_ref[...]
    high[every(3, channels, 4), :] = vectors_ref[...]
    keep_ref[...] = jnp.where(first, low[...], high[...])
    give_ref[...] = jnp.where(first, high[...], low[...])


def beside_rear(grad_normed_ref, hat_t_ref, scale_ref, gain_ref, pair_grad_ref):
    hat = hat_t_ref[...]
    scaled = grad_normed_ref[...] * column(gain_ref[...])
    grad = scale_ref[:1, :] * (
        scaled
        - jnp.mean(scaled, axis=0, keepdims=True)
        - hat * jnp.mean(scaled * hat, axis=0, keepdims=True)
    )
    pair_grad_ref[...] = jnp.transpose(grad).astype(BF16)


def split_vectors(sums, count):
    at = every(3, count, 4)
    values = sums[at, :]
    sums[at, :] = columns(values[:, :1] + values[:, 2:3], values[:, 1:2] + values[:, 3:4])


def add(keep_ref, got_ref, sum_ref, sums):
    sums[...] = keep_ref[...] + got_ref[...]
    split_vectors(sums, sums.shape[0] // 4)
    sum_ref[...] = sums[...].astype(BF16)


def reduce_share(parts_ref, share_ref):
    share_ref[...] = jnp.sum(parts_ref[...].astype(F32).reshape(-1, 8, LANES), axis=0)


def spread(share_ref, got_ref, copies_ref, sums):
    sums[...] = share_ref[...] + got_ref[...]
    split_vectors(sums, 2)
    copies_ref[...] = (
        jnp.broadcast_to(sums[...][None], (copies_ref.shape[0] // 8, 8, LANES))
        .reshape(copies_ref.shape)
        .astype(BF16)
    )


def finish(
    own_ref, other_ref, w_in_ref, w_gate_ref, w_out_ref, in_gain_ref, in_bias_ref, out_gain_ref, out_bias_ref,
    low, high,
):
    first = first_half()
    own, other = own_ref[...].astype(F32), other_ref[...].astype(F32)
    low[...] = jnp.where(first, own, other)
    high[...] = jnp.where(first, other, own)
    channels = w_in_ref.shape[0]
    for t in range(3):
        w_in_ref[:, t * LANES : (t + 1) * LANES] = low[every(t, channels, 4), :]
    w_in_ref[:, 3 * LANES :] = high[every(0, channels, 4), :]
    w_gate_ref[...] = high[every(1, channels, 4), :]
    w_out_ref[...] = high[every(2, channels, 4), :]
    inner = jnp.transpose(low[every(3, channels, 4), :])
    outer = jnp.transpose(high[every(3, channels, 4), :])
    inner, outer = inner[:2] + inner[2:4], outer[:2] + outer[2:4]
    in_gain_ref[...], in_bias_ref[...] = inner[:1], inner[1:2]
    out_gain_ref[...], out_bias_ref[...] = outer[:1], outer[1:2]


def on_device(
    pair, grad_out, w_in, w_gate, w_out, ln_in_gain, ln_in_bias, ln_out_gain, ln_out_bias
):
    shape = pair.shape
    channels = shape[3]
    hidden = w_out.shape[0]
    cells = shape[1] * shape[2]
    full_len = shape[2]
    pair2 = pair.reshape(cells, channels)
    grad2 = grad_out.reshape(cells, channels)
    in_gain_row, in_bias_row = ln_in_gain.reshape(1, -1), ln_in_bias.reshape(1, -1)
    out_gain_row, out_bias_row = ln_out_gain.reshape(1, -1), ln_out_bias.reshape(1, -1)
    grid = (hidden, cells)
    quarter = (4 * hidden, LANES)
    whole = (8 * hidden, LANES)
    to_chips = lambda a: lax.all_to_all(a, CHIPS, 0, 0, tiled=True)
    stay = lambda a: pltpu.with_memory_space_constraint(a, pltpu.HBM)
    swap = lambda a: lax.ppermute(a, "c", SWAP)

    edges, normed, w_in_t = call(
        front, [(whole, BF16), ((cells, channels), BF16), ((4 * hidden, channels), BF16)],
        [
            whole, pltpu.VMEM((cells, channels), BF16), pltpu.VMEM(w_in.shape, BF16), (1, channels), (1, channels),
            pltpu.SemaphoreType.DMA((4,)),
        ],
        far=4,
    )(stay(pair2), stay(in_gain_row), stay(in_bias_row), stay(w_in))
    own, normed = lax.optimization_barrier((to_chips(edges), normed))
    other = swap(own)
    normed_t, hat_t, scale, factors, grad_t, gate_t, grad_lin, grad_out_normed, scaled, mean = call(
        beside_front,
        [
            (grid, BF16), (grid, F32), ((8, cells), F32), ((4 * hidden, cells), F32), (grid, F32), (grid, F32),
            (grid, BF16), (grid, F32), (grid, F32), ((8, cells), F32),
        ],
        work=1 << 28,
    )(normed, pair2, grad2, w_in_t, w_gate, w_out, out_gain_row)
    other, normed_t = lax.optimization_barrier((other, normed_t))
    product, left, right = call(
        contract,
        [(quarter, BF16), ((2, full_len // 2, full_len), BF16), ((2, full_len, full_len), BF16)],
        [whole, whole, quarter, quarter],
    )(own, other)
    product = to_chips(product)
    (grad_product,) = call(middle, [(quarter, BF16)], [quarter, quarter])(product, scaled, mean)
    grad_cols = to_chips(grad_product)
    grad_left, keep, give = call(contract_back, [(quarter, F32)] * 3, [quarter, quarter])(
        grad_cols, left, right
    )
    give, product = lax.optimization_barrier((give, product))
    got = swap(give)
    w_out_part, w_gate_part, vectors, gate_term = call(
        beside_middle,
        [((hidden, channels), F32), ((channels, channels), F32), ((hidden, LANES), F32), (grid, F32)],
        [quarter],
        work=1 << 28,
    )(product, grad_out_normed, grad_lin, grad_t, gate_t, normed_t, w_out, w_gate, out_gain_row, out_bias_row)
    got, vectors = lax.optimization_barrier((got, vectors))
    (grad_edges,) = call(join, [(whole, BF16)])(grad_left, keep, got)
    grad_edges = to_chips(grad_edges)
    keep, give, grad_normed = call(
        rear, [(quarter, F32), (quarter, F32), (grid, F32)], [quarter] * 4
    )(grad_edges, factors, normed_t, hat_t, w_in, gate_term, w_out_part, w_gate_part, vectors)
    (parts,) = call(add, [(quarter, BF16)], [quarter])(keep, swap(give))
    (share,) = call(reduce_share, [((8, LANES), F32)])(to_chips(parts))
    share, grad_normed = lax.optimization_barrier((share, grad_normed))
    got = lax.ppermute(share, ("X", "c"), [(0, 3), (1, 2), (2, 1), (3, 0)])
    (pair_grad,) = call(beside_rear, [((cells, channels), BF16)], work=1 << 28)(
        grad_normed, hat_t, scale, in_gain_row
    )
    got, pair_grad = lax.optimization_barrier((got, pair_grad))
    (copies,) = call(spread, [(quarter, BF16)], [(8, LANES)])(share, got)
    mine = to_chips(copies)
    w_in_total, w_gate_total, w_out_total, *vectors = call(
        finish,
        [(w_in.shape, F32), (w_gate.shape, F32), (w_out.shape, F32)] + [((1, LANES), F32)] * 4,
        [quarter, quarter],
    )(mine, swap(mine))
    return (
        pair_grad.reshape(shape),
        w_in_total,
        w_gate_total,
        w_out_total,
        *(vector.reshape(-1) for vector in vectors),
    )


def solution(mesh):
    fine = Mesh(mesh.devices.reshape(2, 2, 8, 4, 2), ("X", "x", "z", "y", "c"))
    cells = P("X", ("x", "z", "y", "c"), None, None)
    in_specs = (cells, cells, P(), P(), P(), P(), P(), P(), P())
    out_specs = (cells, P(), P(), P(), P(), P(), P(), P())
    return jax.shard_map(
        on_device, mesh=fine, in_specs=in_specs, out_specs=out_specs, check_vma=False
    )
```

```python
import functools

import jax
import jax.numpy as jnp
from jax import lax
from jax.experimental import pallas as pl
from jax.experimental.pallas import tpu as pltpu
from jax.sharding import Mesh, PartitionSpec as P

EPSILON = 1e-05
CHIPS = ("x", "z", "y")
SWAP = [(0, 1), (1, 0)]
LANES = 128
F32 = jnp.float32
BF16 = jnp.bfloat16


def call(body, outs, scratch=(), work=0, far=0):
    def run(*operands):
        return pl.pallas_call(
            body,
            out_shape=[jax.ShapeDtypeStruct(shape, dtype) for shape, dtype in outs],
            in_specs=[pl.BlockSpec(memory_space=pltpu.HBM)] * far
            + [pl.BlockSpec(memory_space=pltpu.VMEM)] * (len(operands) - far),
            out_specs=[pl.BlockSpec(memory_space=pltpu.VMEM)] * len(outs),
            scratch_shapes=[pltpu.VMEM(s, F32) if isinstance(s, tuple) else s for s in scratch],
            compiler_params=pltpu.CompilerParams(vmem_limit_bytes=8 * 1024 * 1024),
            cost_estimate=pl.CostEstimate(
                flops=work, bytes_accessed=1 << 20, transcendentals=0
            ),
        )(*operands)

    return run


def dot_nt(a, b):
    return lax.dot_general(a, b, (((1,), (1,)), ((), ())), preferred_element_type=F32)


def dot_nn(a, b):
    return lax.dot_general(a, b, (((1,), (0,)), ((), ())), preferred_element_type=F32)


def sigmoid(x):
    return jax.nn.sigmoid(x)


def first_half():
    return lax.axis_index("c") == lax.axis_index("X")


def every(start, count, stride):
    return pl.ds(start, count, stride=stride)


def column(row):
    return jnp.transpose(jnp.broadcast_to(row, (LANES, row.shape[1])))[:, :1]


def front(
    pair_far, gain_far, bias_far, w_in_far, out_gain_far, out_bias_far, edges_ref, normed_ref, w_in_t_ref, norms_ref,
    rows, pair_ref, w_in_ref, gain_ref, bias_ref, out_gain_ref, out_bias_ref, arrived,
):
    copies = [
        pltpu.make_async_copy(source, target, arrived.at[n])
        for n, (source, target) in enumerate(
            [(pair_far, pair_ref), (gain_far, gain_ref), (bias_far, bias_ref), (w_in_far, w_in_ref),
             (out_gain_far, out_gain_ref), (out_bias_far, out_bias_ref)]
        )
    ]
    for copy in copies:
        copy.start()
    for copy in copies[:3]:
        copy.wait()
    values = pair_ref[...].astype(F32)
    center = values - jnp.mean(values, axis=1, keepdims=True)
    scale = lax.rsqrt(jnp.mean(center * center, axis=1, keepdims=True) + EPSILON)
    normed = (center * scale * gain_ref[...] + bias_ref[...]).astype(BF16)
    normed_ref[...] = normed
    for copy in copies[3:]:
        copy.wait()
    norms = [gain_ref[...], bias_ref[...], out_gain_ref[...], out_bias_ref[...]]
    norms_ref[...] = jnp.concatenate(norms + norms, axis=0)
    w_in_t = jnp.transpose(w_in_ref[...].astype(F32)).astype(BF16)
    w_in_t_ref[...] = w_in_t
    hidden = w_in_t.shape[0] // 4
    for side in range(2):
        proj = dot_nt(w_in_t[2 * side * hidden : (2 * side + 1) * hidden], normed)
        gate = dot_nt(w_in_t[(2 * side + 1) * hidden : (2 * side + 2) * hidden], normed)
        value = sigmoid(gate) * proj
        for u in range(4):
            rows[every(4 * side + u, hidden, 8), :] = value[:, u * LANES : (u + 1) * LANES]
    edges_ref[...] = rows[...].astype(BF16)


def beside_front(
    normed_ref, pair_ref, grad_ref, w_in_t_ref, w_gate_ref, w_out_ref, norms_ref,
    normed_t_ref, hat_t_ref, scale_ref, factors_ref, grad_t_ref, gate_t_ref, grad_lin_ref,
    grad_out_normed_ref, scaled_ref, mean_ref,
):
    hidden = w_out_ref.shape[0]
    normed = normed_ref[...]
    normed_t_ref[...] = jnp.transpose(normed.astype(F32)).astype(BF16)
    values = jnp.transpose(pair_ref[...].astype(F32))
    center = values - jnp.mean(values, axis=0, keepdims=True)
    scale = lax.rsqrt(jnp.mean(center * center, axis=0, keepdims=True) + EPSILON)
    hat_t_ref[...] = center * scale
    scale_ref[...] = jnp.broadcast_to(scale, scale_ref.shape)
    grad_t = jnp.transpose(grad_ref[...].astype(F32))
    grad_t_ref[...] = grad_t
    w_gate_t = jnp.transpose(w_gate_ref[...].astype(F32)).astype(BF16)
    gate = sigmoid(dot_nt(w_gate_t, normed))
    gate_t_ref[...] = gate
    grad_lin = (grad_t * gate).astype(BF16)
    grad_lin_ref[...] = grad_lin
    grad_out_normed = dot_nn(w_out_ref[...], grad_lin)
    grad_out_normed_ref[...] = grad_out_normed
    scaled = grad_out_normed * column(norms_ref[2:3, :])
    scaled_ref[...] = scaled
    mean_ref[...] = jnp.broadcast_to(jnp.mean(scaled, axis=0, keepdims=True), mean_ref.shape)
    factors_ref[...] = factors_of(w_in_t_ref, normed)


def factors_of(w_in_t_ref, normed):
    hidden = w_in_t_ref.shape[0] // 4
    at = pl.multiple_of(jnp.where(first_half(), 0, 2 * hidden), LANES)
    proj = dot_nt(w_in_t_ref[pl.ds(at, hidden), :], normed)
    sig = sigmoid(dot_nt(w_in_t_ref[pl.ds(at + hidden, hidden), :], normed))
    return jnp.concatenate([sig, proj * sig * (1.0 - sig)], axis=0)


def beside_back(
    pair_ref, norms_ref, w_in_t_ref, normed_t_ref, hat_t_ref, factors_ref,
    both_normed_ref, both_hat_ref, both_factors_ref,
):
    core = lax.axis_index("c")
    cells = pair_ref.shape[0]
    values = pair_ref[...].astype(F32)
    center = values - jnp.mean(values, axis=1, keepdims=True)
    hat = center * lax.rsqrt(jnp.mean(center * center, axis=1, keepdims=True) + EPSILON)
    normed = (hat * norms_ref[:1, :] + norms_ref[1:2, :]).astype(BF16)
    for both_ref, own, other in [
        (both_normed_ref, normed_t_ref[...].astype(F32), jnp.transpose(normed.astype(F32))),
        (both_hat_ref, hat_t_ref[...], jnp.transpose(hat)),
        (both_factors_ref, factors_ref[...], factors_of(w_in_t_ref, normed)),
    ]:
        both_ref[:, :cells] = jnp.where(core == 0, own, other).astype(both_ref.dtype)
        both_ref[:, cells:] = jnp.where(core == 0, other, own).astype(both_ref.dtype)


def contract(own_ref, other_ref, product_ref, left_ref, right_ref, own, other, natural, rows):
    core = lax.axis_index("c")
    own[...] = own_ref[...].astype(F32)
    other[...] = other_ref[...].astype(F32)
    chips = own.shape[0] // 16
    for ch in range(2):
        halves = []
        for kh in range(2):
            halves.append(
                jnp.concatenate([own[every(ch * 8 + 2 * r + kh, chips, 16), :] for r in range(2)], axis=0)
            )
            for r in range(2):
                at = every(ch * 8 + 4 + 2 * r + kh, chips, 16)
                mine, theirs = own[at, :], other[at, :]
                base = kh * 4 * chips + r
                natural[every(base, chips, 4), :] = jnp.where(core == 0, mine, theirs)
                natural[every(base + 2, chips, 4), :] = jnp.where(core == 0, theirs, mine)
        left = jnp.concatenate(halves, axis=1).astype(BF16)
        right = jnp.concatenate([natural[: 4 * chips, :], natural[4 * chips :, :]], axis=1).astype(BF16)
        left_ref[ch, : 2 * chips] = left
        theirs = [
            jnp.concatenate([other[every(ch * 8 + 2 * r + kh, chips, 16), :] for r in range(2)], axis=0)
            for kh in range(2)
        ]
        left_ref[ch, 2 * chips :] = jnp.concatenate(theirs, axis=1).astype(BF16)
        right_ref[ch] = right
        product = dot_nt(left, right)
        for r in range(2):
            for jh in range(2):
                rows[every(ch * 4 + 2 * r + jh, chips, 8), :] = product[
                    r * chips : (r + 1) * chips, jh * LANES : (jh + 1) * LANES
                ]
    product_ref[...] = rows[...].astype(BF16)


def out_norm(values):
    center = values - jnp.mean(values, axis=0, keepdims=True)
    scale = lax.rsqrt(jnp.mean(center * center, axis=0, keepdims=True) + EPSILON)
    return center * scale, scale


def middle(product_ref, scaled_ref, mean_ref, grad_ref, rows, grads):
    hidden = scaled_ref.shape[0]
    rows[...] = product_ref[...].astype(F32)
    for u in range(4):
        hat, scale = out_norm(rows[every(u, hidden, 4), :])
        at = slice(u * LANES, (u + 1) * LANES)
        scaled = scaled_ref[:, at]
        both = jnp.mean(scaled * hat, axis=0, keepdims=True)
        grads[every(u, hidden, 4), :] = scale * (scaled - mean_ref[:1, at] - hat * both)
    grad_ref[...] = grads[...].astype(BF16)


def beside_middle(
    product_ref, grad_out_normed_ref, grad_lin_ref, grad_t_ref, gate_t_ref, normed_t_ref,
    w_out_ref, w_gate_ref, norms_ref, keep_ref, give_ref, vectors_ref, gate_term_ref,
    rows,
):
    hidden = w_out_ref.shape[0]
    rows[...] = product_ref[...].astype(F32)
    hats, normed = [], []
    gain, bias = column(norms_ref[2:3, :]), column(norms_ref[3:4, :])
    for u in range(4):
        hat, _ = out_norm(rows[every(u, hidden, 4), :])
        hats.append(hat)
        normed.append((hat * gain + bias).astype(BF16))
    hat = jnp.concatenate(hats, axis=1)
    out_normed = jnp.concatenate(normed, axis=1)
    w_out_t = jnp.transpose(w_out_ref[...].astype(F32)).astype(BF16)
    outlin = dot_nn(w_out_t, out_normed)
    gate = gate_t_ref[...]
    grad_gate = (grad_t_ref[...] * outlin * gate * (1.0 - gate)).astype(BF16)
    first = first_half()
    w_out_part = dot_nt(out_normed, grad_lin_ref[...])
    w_gate_part = dot_nt(normed_t_ref[...], grad_gate)
    keep_ref[...] = jnp.where(first, w_gate_part, w_out_part)
    give_ref[...] = jnp.where(first, w_out_part, w_gate_part)
    gate_term_ref[...] = dot_nn(w_gate_ref[...], grad_gate)
    grad_out_normed = grad_out_normed_ref[...]
    lane = lax.broadcasted_iota(jnp.int32, vectors_ref.shape, 1)
    vectors_ref[...] = jnp.where(
        lane == 0,
        jnp.sum(grad_out_normed * hat, axis=1, keepdims=True),
        jnp.sum(grad_out_normed, axis=1, keepdims=True),
    )


def columns(*sums):
    lane = lax.broadcasted_iota(jnp.int32, (sums[0].shape[0], LANES), 1)
    high = [value.astype(BF16).astype(F32) for value in sums]
    out = jnp.zeros(lane.shape, F32)
    for n, value in enumerate(high + [value - top for value, top in zip(sums, high)]):
        out = jnp.where(lane == n, value, out)
    return out


def contract_back(grad_ref, other_ref, left_ref, right_ref, edges_ref, own, other, natural, edges):
    core, first = lax.axis_index("c"), first_half()
    own[...] = grad_ref[...].astype(F32)
    other[...] = other_ref[...].astype(F32)
    chips = own.shape[0] // 8
    for ch in range(2):
        halves = []
        for jh in range(2):
            halves.append(
                jnp.concatenate(
                    [rows[every(ch * 4 + 2 * r + jh, chips, 8), :] for rows in (own, other) for r in range(2)], axis=0
                )
            )
        grad = jnp.concatenate(halves, axis=1)
        grad_right = dot_nn(jnp.transpose(grad).astype(BF16), left_ref[ch])
        grad_left = dot_nn(grad.astype(BF16), right_ref[ch])
        natural[: 4 * chips, :] = grad_right[:, :LANES]
        natural[4 * chips :, :] = grad_right[:, LANES:]
        for c in range(2):
            for r in range(2):
                for kh in range(2):
                    at = slice(kh * LANES, (kh + 1) * LANES)
                    mine = grad_left[r * chips : (r + 1) * chips, at]
                    theirs = grad_left[(2 + r) * chips : (3 + r) * chips, at]
                    edges[every(ch * 8 + 4 * c + 2 * r + kh, chips, 16), :] = jnp.where(
                        first,
                        jnp.where(core == c, mine, theirs),
                        natural[every(kh * 4 * chips + 2 * c + r, chips, 4), :],
                    )
    edges_ref[...] = edges[...].astype(BF16)


def rear(
    edges_ref, factors_ref, normed_t_ref, hat_t_ref, w_in_ref, gate_term_ref, keep_ref, got_ref, vectors_ref,
    parts_ref, grad_normed_ref, give_ref, rows, parts,
):
    core, first = lax.axis_index("c"), first_half()
    hidden = w_in_ref.shape[1] // 4
    cells = gate_term_ref.shape[1]
    rows[...] = edges_ref[...].astype(F32)
    pieces = []
    for u in range(8):
        at = slice(u * LANES, (u + 1) * LANES)
        grad = rows[every(u, hidden, 8), :]
        pieces.append(
            jnp.concatenate([grad * factors_ref[:hidden, at], grad * factors_ref[hidden:, at]], axis=0).astype(BF16)
        )
    grad_projected = jnp.concatenate(pieces, axis=1)
    w_in_part = dot_nt(normed_t_ref[...], grad_projected)
    w_in = w_in_ref[...].astype(F32)
    w_in = jnp.where(first, w_in[:, : 2 * hidden], w_in[:, 2 * hidden :]).astype(BF16)
    grad_normed = dot_nn(w_in, grad_projected)
    low, high = grad_normed[:, :cells], grad_normed[:, cells:]
    gate_term = gate_term_ref[...]
    low = low + jnp.where(core == 0, gate_term, 0.0)
    high = high + jnp.where(core == 0, 0.0, gate_term)
    grad_normed_ref[...] = jnp.where(core == 0, low, high)
    give_ref[...] = jnp.where(core == 0, high, low)
    channels = w_in_part.shape[0]
    for t in range(2):
        parts[every(t, channels, 4), :] = w_in_part[:, t * LANES : (t + 1) * LANES]
    parts[every(2, channels, 4), :] = keep_ref[...] + got_ref[...]
    gain = jnp.sum(low * hat_t_ref[:, :cells] + high * hat_t_ref[:, cells:], axis=1, keepdims=True)
    parts[every(3, channels, 4), :] = columns(
        gain, jnp.sum(low + high, axis=1, keepdims=True), vectors_ref[:, :1], vectors_ref[:, 1:2]
    )
    parts_ref[...] = parts[...].astype(BF16)


def beside_rear(grad_normed_ref, got_ref, hat_t_ref, scale_ref, norms_ref, pair_grad_ref):
    hat = hat_t_ref[...]
    scaled = (grad_normed_ref[...] + got_ref[...]) * column(norms_ref[:1, :])
    grad = scale_ref[:1, :] * (
        scaled
        - jnp.mean(scaled, axis=0, keepdims=True)
        - hat * jnp.mean(scaled * hat, axis=0, keepdims=True)
    )
    pair_grad_ref[...] = jnp.transpose(grad).astype(BF16)


def split_vectors(sums, count):
    at = every(3, count, 4)
    values = sums[at, :]
    sums[at, :] = columns(*(values[:, n : n + 1] + values[:, n + 4 : n + 5] for n in range(4)))


def reduce_share(parts_ref, share_ref):
    share_ref[...] = jnp.sum(parts_ref[...].astype(F32).reshape(-1, 8, LANES), axis=0)


def spread(share_ref, got_ref, copies_ref, sums):
    sums[...] = share_ref[...] + got_ref[...]
    split_vectors(sums, 2)
    copies_ref[...] = (
        jnp.broadcast_to(sums[...][None], (copies_ref.shape[0] // 8, 8, LANES))
        .reshape(copies_ref.shape)
        .astype(BF16)
    )


def finish(
    own_ref, other_ref, w_in_ref, w_gate_ref, w_out_ref, in_gain_ref, in_bias_ref, out_gain_ref, out_bias_ref,
    low, high,
):
    first = first_half()
    own, other = own_ref[...].astype(F32), other_ref[...].astype(F32)
    low[...] = jnp.where(first, own, other)
    high[...] = jnp.where(first, other, own)
    channels = w_in_ref.shape[0]
    for t in range(2):
        w_in_ref[:, t * LANES : (t + 1) * LANES] = low[every(t, channels, 4), :]
        w_in_ref[:, (2 + t) * LANES : (3 + t) * LANES] = high[every(t, channels, 4), :]
    w_gate_ref[...] = low[every(2, channels, 4), :]
    w_out_ref[...] = high[every(2, channels, 4), :]
    sums = jnp.transpose(low[every(3, channels, 4), :] + high[every(3, channels, 4), :])
    sums = sums[:4] + sums[4:8]
    in_gain_ref[...], in_bias_ref[...] = sums[:1], sums[1:2]
    out_gain_ref[...], out_bias_ref[...] = sums[2:3], sums[3:4]


def on_device(
    pair, grad_out, w_in, w_gate, w_out, ln_in_gain, ln_in_bias, ln_out_gain, ln_out_bias
):
    shape = pair.shape
    channels = shape[3]
    hidden = w_out.shape[0]
    cells = shape[1] * shape[2]
    full_len = shape[2]
    pair2 = pair.reshape(cells, channels)
    grad2 = grad_out.reshape(cells, channels)
    in_gain_row, in_bias_row = ln_in_gain.reshape(1, -1), ln_in_bias.reshape(1, -1)
    out_gain_row, out_bias_row = ln_out_gain.reshape(1, -1), ln_out_bias.reshape(1, -1)
    grid = (hidden, cells)
    quarter = (4 * hidden, LANES)
    whole = (8 * hidden, LANES)
    to_chips = lambda a: lax.all_to_all(a, CHIPS, 0, 0, tiled=True)
    stay = lambda a: pltpu.with_memory_space_constraint(a, pltpu.HBM)
    swap = lambda a: lax.ppermute(a, "c", SWAP)

    edges, normed, w_in_t, norms = call(
        front, [(whole, BF16), ((cells, channels), BF16), ((4 * hidden, channels), BF16), ((8, LANES), F32)],
        [
            whole, pltpu.VMEM((cells, channels), BF16), pltpu.VMEM(w_in.shape, BF16), (1, channels), (1, channels),
            (1, channels), (1, channels),
            pltpu.SemaphoreType.DMA((6,)),
        ],
        far=6,
    )(stay(pair2), stay(in_gain_row), stay(in_bias_row), stay(w_in), stay(out_gain_row), stay(out_bias_row))
    own, normed, pair_again = lax.optimization_barrier((to_chips(edges), normed, pair2))
    other = swap(own)
    pair_other = swap(pair_again)
    normed_t, hat_t, scale, factors, grad_t, gate_t, grad_lin, grad_out_normed, scaled, mean = call(
        beside_front,
        [
            (grid, BF16), (grid, F32), ((8, cells), F32), ((2 * hidden, cells), F32), (grid, F32), (grid, F32),
            (grid, BF16), (grid, F32), (grid, F32), ((8, cells), F32),
        ],
        work=1 << 28,
    )(normed, pair2, grad2, w_in_t, w_gate, w_out, norms)
    other, normed_t, pair_other = lax.optimization_barrier((other, normed_t, pair_other))
    product, left, right = call(
        contract,
        [(quarter, BF16), ((2, full_len, full_len), BF16), ((2, full_len, full_len), BF16)],
        [whole, whole, quarter, quarter],
    )(own, other)
    product = to_chips(product)
    (grad_product,) = call(middle, [(quarter, BF16)], [quarter, quarter])(product, scaled, mean)
    grad_cols = to_chips(grad_product)
    grad_cols, product, pair_other = lax.optimization_barrier((grad_cols, product, pair_other))
    grad_other = swap(grad_cols)
    keep, give, vectors, gate_term = call(
        beside_middle,
        [((hidden, channels), F32), ((channels, channels), F32), ((hidden, LANES), F32), (grid, F32)],
        [quarter],
        work=1 << 28,
    )(product, grad_out_normed, grad_lin, grad_t, gate_t, normed_t, w_out, w_gate, norms)
    both = (channels, 2 * cells)
    both_normed, both_hat, both_factors = call(
        beside_back, [(both, BF16), (both, F32), ((2 * hidden, 2 * cells), F32)], work=1 << 28
    )(pair_other, norms, w_in_t, normed_t, hat_t, factors)
    grad_other, gate_term, both_hat = lax.optimization_barrier((grad_other, gate_term, both_hat))
    got = swap(give)
    (grad_edges,) = call(contract_back, [(whole, BF16)], [quarter, quarter, quarter, whole])(
        grad_cols, grad_other, left, right
    )
    grad_edges, got = lax.optimization_barrier((grad_edges, got))
    grad_edges = to_chips(grad_edges)
    parts, grad_normed, give = call(
        rear, [(quarter, BF16), (grid, F32), (grid, F32)], [whole, quarter]
    )(grad_edges, both_factors, both_normed, both_hat, w_in, gate_term, keep, got, vectors)
    (share,) = call(reduce_share, [((8, LANES), F32)])(to_chips(parts))
    share, give = lax.optimization_barrier((share, give))
    got = lax.ppermute(share, ("X", "c"), [(0, 3), (1, 2), (2, 1), (3, 0)])
    (pair_grad,) = call(beside_rear, [((cells, channels), BF16)], work=1 << 28)(
        grad_normed, swap(give), hat_t, scale, norms
    )
    got, pair_grad = lax.optimization_barrier((got, pair_grad))
    (copies,) = call(spread, [(quarter, BF16)], [(8, LANES)])(share, got)
    mine = to_chips(copies)
    w_in_total, w_gate_total, w_out_total, *vectors = call(
        finish,
        [(w_in.shape, F32), (w_gate.shape, F32), (w_out.shape, F32)] + [((1, LANES), F32)] * 4,
        [quarter, quarter],
    )(mine, swap(mine))
    return (
        pair_grad.reshape(shape),
        w_in_total,
        w_gate_total,
        w_out_total,
        *(vector.reshape(-1) for vector in vectors),
    )


def solution(mesh):
    fine = Mesh(mesh.devices.reshape(2, 2, 8, 4, 2), ("X", "x", "z", "y", "c"))
    cells = P("X", ("x", "z", "y", "c"), None, None)
    in_specs = (cells, cells, P(), P(), P(), P(), P(), P(), P())
    out_specs = (cells, P(), P(), P(), P(), P(), P(), P())
    return jax.shard_map(
        on_device, mesh=fine, in_specs=in_specs, out_specs=out_specs, check_vma=False
    )
```

```python
import functools

import jax
import jax.numpy as jnp
from jax import lax
from jax.experimental import pallas as pl
from jax.experimental.pallas import tpu as pltpu
from jax.sharding import Mesh, PartitionSpec as P

EPSILON = 1e-05
CHIPS = ("x", "z", "y")
SWAP = [(0, 1), (1, 0)]
LANES = 128
F32 = jnp.float32
BF16 = jnp.bfloat16


def call(body, outs, scratch=(), work=0, far=0):
    def run(*operands):
        return pl.pallas_call(
            body,
            out_shape=[jax.ShapeDtypeStruct(shape, dtype) for shape, dtype in outs],
            in_specs=[pl.BlockSpec(memory_space=pltpu.HBM)] * far
            + [pl.BlockSpec(memory_space=pltpu.VMEM)] * (len(operands) - far),
            out_specs=[pl.BlockSpec(memory_space=pltpu.VMEM)] * len(outs),
            scratch_shapes=[pltpu.VMEM(s, F32) if isinstance(s, tuple) else s for s in scratch],
            compiler_params=pltpu.CompilerParams(vmem_limit_bytes=8 * 1024 * 1024),
            cost_estimate=pl.CostEstimate(
                flops=work, bytes_accessed=1 << 20, transcendentals=0
            ),
        )(*operands)

    return run


def dot_nt(a, b):
    return lax.dot_general(a, b, (((1,), (1,)), ((), ())), preferred_element_type=F32)


def dot_nn(a, b):
    return lax.dot_general(a, b, (((1,), (0,)), ((), ())), preferred_element_type=F32)


def sigmoid(x):
    return jax.nn.sigmoid(x)


def first_half():
    return lax.axis_index("c") == lax.axis_index("X")


def every(start, count, stride):
    return pl.ds(start, count, stride=stride)


def column(row):
    return jnp.transpose(jnp.broadcast_to(row, (LANES, row.shape[1])))[:, :1]


def front(
    pair_far, gain_far, bias_far, w_in_far, out_gain_far, out_bias_far, edges_ref, normed_ref, w_in_t_ref, norms_ref,
    rows, pair_ref, w_in_ref, gain_ref, bias_ref, out_gain_ref, out_bias_ref, arrived,
):
    copies = [
        pltpu.make_async_copy(source, target, arrived.at[n])
        for n, (source, target) in enumerate(
            [(pair_far, pair_ref), (gain_far, gain_ref), (bias_far, bias_ref), (w_in_far, w_in_ref),
             (out_gain_far, out_gain_ref), (out_bias_far, out_bias_ref)]
        )
    ]
    for copy in copies:
        copy.start()
    for copy in copies[:3]:
        copy.wait()
    values = pair_ref[...].astype(F32)
    center = values - jnp.mean(values, axis=1, keepdims=True)
    scale = lax.rsqrt(jnp.mean(center * center, axis=1, keepdims=True) + EPSILON)
    normed = (center * scale * gain_ref[...] + bias_ref[...]).astype(BF16)
    normed_ref[...] = normed
    for copy in copies[3:]:
        copy.wait()
    norms = [gain_ref[...], bias_ref[...], out_gain_ref[...], out_bias_ref[...]]
    norms_ref[...] = jnp.concatenate(norms + norms, axis=0)
    w_in_t = jnp.transpose(w_in_ref[...].astype(F32)).astype(BF16)
    w_in_t_ref[...] = w_in_t
    hidden = w_in_t.shape[0] // 4
    for side in range(2):
        proj = dot_nt(w_in_t[2 * side * hidden : (2 * side + 1) * hidden], normed)
        gate = dot_nt(w_in_t[(2 * side + 1) * hidden : (2 * side + 2) * hidden], normed)
        value = sigmoid(gate) * proj
        for u in range(4):
            rows[every(4 * side + u, hidden, 8), :] = value[:, u * LANES : (u + 1) * LANES]
    edges_ref[...] = rows[...].astype(BF16)


def beside_front(
    normed_ref, pair_ref, grad_ref, w_in_t_ref, w_gate_ref, w_out_ref, norms_ref,
    normed_t_ref, hat_t_ref, scale_ref, factors_ref, grad_t_ref, gate_t_ref, grad_lin_ref,
    grad_out_normed_ref, scaled_ref, mean_ref,
):
    hidden = w_out_ref.shape[0]
    normed = normed_ref[...]
    normed_t_ref[...] = jnp.transpose(normed.astype(F32)).astype(BF16)
    values = jnp.transpose(pair_ref[...].astype(F32))
    center = values - jnp.mean(values, axis=0, keepdims=True)
    scale = lax.rsqrt(jnp.mean(center * center, axis=0, keepdims=True) + EPSILON)
    hat_t_ref[...] = center * scale
    scale_ref[...] = jnp.broadcast_to(scale, scale_ref.shape)
    grad_t = jnp.transpose(grad_ref[...].astype(F32))
    grad_t_ref[...] = grad_t
    w_gate_t = jnp.transpose(w_gate_ref[...].astype(F32)).astype(BF16)
    gate = sigmoid(dot_nt(w_gate_t, normed))
    gate_t_ref[...] = gate
    grad_lin = (grad_t * gate).astype(BF16)
    grad_lin_ref[...] = grad_lin
    grad_out_normed = dot_nn(w_out_ref[...], grad_lin)
    grad_out_normed_ref[...] = grad_out_normed
    scaled = grad_out_normed * column(norms_ref[2:3, :])
    scaled_ref[...] = scaled
    mean_ref[...] = jnp.broadcast_to(jnp.mean(scaled, axis=0, keepdims=True), mean_ref.shape)
    factors_ref[...] = factors_of(w_in_t_ref, normed)


def factors_of(w_in_t_ref, normed):
    hidden = w_in_t_ref.shape[0] // 4
    at = pl.multiple_of(jnp.where(first_half(), 0, 2 * hidden), LANES)
    proj = dot_nt(w_in_t_ref[pl.ds(at, hidden), :], normed)
    sig = sigmoid(dot_nt(w_in_t_ref[pl.ds(at + hidden, hidden), :], normed))
    return jnp.concatenate([sig, proj * sig * (1.0 - sig)], axis=0)


def beside_back(
    pair_ref, norms_ref, w_in_t_ref, normed_t_ref, hat_t_ref, factors_ref,
    both_normed_ref, both_hat_ref, both_factors_ref,
):
    core = lax.axis_index("c")
    cells = pair_ref.shape[0]
    values = pair_ref[...].astype(F32)
    center = values - jnp.mean(values, axis=1, keepdims=True)
    hat = center * lax.rsqrt(jnp.mean(center * center, axis=1, keepdims=True) + EPSILON)
    normed = (hat * norms_ref[:1, :] + norms_ref[1:2, :]).astype(BF16)
    for both_ref, own, other in [
        (both_normed_ref, normed_t_ref[...].astype(F32), jnp.transpose(normed.astype(F32))),
        (both_hat_ref, hat_t_ref[...], jnp.transpose(hat)),
        (both_factors_ref, factors_ref[...], factors_of(w_in_t_ref, normed)),
    ]:
        both_ref[:, :cells] = jnp.where(core == 0, own, other).astype(both_ref.dtype)
        both_ref[:, cells:] = jnp.where(core == 0, other, own).astype(both_ref.dtype)


def contract(own_ref, other_ref, product_ref, left_ref, right_ref, own, other, natural, rows):
    core = lax.axis_index("c")
    own[...] = own_ref[...].astype(F32)
    other[...] = other_ref[...].astype(F32)
    chips = own.shape[0] // 16
    for ch in range(2):
        halves = []
        for kh in range(2):
            halves.append(
                jnp.concatenate([own[every(ch * 8 + 2 * r + kh, chips, 16), :] for r in range(2)], axis=0)
            )
            for r in range(2):
                at = every(ch * 8 + 4 + 2 * r + kh, chips, 16)
                mine, theirs = own[at, :], other[at, :]
                base = kh * 4 * chips + r
                natural[every(base, chips, 4), :] = jnp.where(core == 0, mine, theirs)
                natural[every(base + 2, chips, 4), :] = jnp.where(core == 0, theirs, mine)
        left = jnp.concatenate(halves, axis=1).astype(BF16)
        right = jnp.concatenate([natural[: 4 * chips, :], natural[4 * chips :, :]], axis=1).astype(BF16)
        left_ref[ch, : 2 * chips] = left
        theirs = [
            jnp.concatenate([other[every(ch * 8 + 2 * r + kh, chips, 16), :] for r in range(2)], axis=0)
            for kh in range(2)
        ]
        left_ref[ch, 2 * chips :] = jnp.concatenate(theirs, axis=1).astype(BF16)
        right_ref[ch] = right
        product = dot_nt(left, right)
        for r in range(2):
            for jh in range(2):
                rows[every(ch * 4 + 2 * r + jh, chips, 8), :] = product[
                    r * chips : (r + 1) * chips, jh * LANES : (jh + 1) * LANES
                ]
    product_ref[...] = rows[...].astype(BF16)


def out_norm(values):
    center = values - jnp.mean(values, axis=0, keepdims=True)
    scale = lax.rsqrt(jnp.mean(center * center, axis=0, keepdims=True) + EPSILON)
    return center * scale, scale


def middle(product_ref, scaled_ref, mean_ref, grad_ref, rows, grads):
    hidden = scaled_ref.shape[0]
    rows[...] = product_ref[...].astype(F32)
    for u in range(4):
        hat, scale = out_norm(rows[every(u, hidden, 4), :])
        at = slice(u * LANES, (u + 1) * LANES)
        scaled = scaled_ref[:, at]
        both = jnp.mean(scaled * hat, axis=0, keepdims=True)
        grads[every(u, hidden, 4), :] = scale * (scaled - mean_ref[:1, at] - hat * both)
    grad_ref[...] = grads[...].astype(BF16)


def beside_middle(
    product_ref, grad_out_normed_ref, grad_lin_ref, grad_t_ref, gate_t_ref, normed_t_ref,
    w_out_ref, w_gate_ref, norms_ref, keep_ref, give_ref, vectors_ref, gate_term_ref,
    rows,
):
    hidden = w_out_ref.shape[0]
    rows[...] = product_ref[...].astype(F32)
    hats, normed = [], []
    gain, bias = column(norms_ref[2:3, :]), column(norms_ref[3:4, :])
    for u in range(4):
        hat, _ = out_norm(rows[every(u, hidden, 4), :])
        hats.append(hat)
        normed.append((hat * gain + bias).astype(BF16))
    hat = jnp.concatenate(hats, axis=1)
    out_normed = jnp.concatenate(normed, axis=1)
    w_out_t = jnp.transpose(w_out_ref[...].astype(F32)).astype(BF16)
    outlin = dot_nn(w_out_t, out_normed)
    gate = gate_t_ref[...]
    grad_gate = (grad_t_ref[...] * outlin * gate * (1.0 - gate)).astype(BF16)
    first = first_half()
    w_out_part = dot_nt(out_normed, grad_lin_ref[...])
    w_gate_part = dot_nt(normed_t_ref[...], grad_gate)
    keep_ref[...] = jnp.where(first, w_gate_part, w_out_part)
    give_ref[...] = jnp.where(first, w_out_part, w_gate_part)
    gate_term_ref[...] = dot_nn(w_gate_ref[...], grad_gate)
    grad_out_normed = grad_out_normed_ref[...]
    lane = lax.broadcasted_iota(jnp.int32, vectors_ref.shape, 1)
    vectors_ref[...] = jnp.where(
        lane == 0,
        jnp.sum(grad_out_normed * hat, axis=1, keepdims=True),
        jnp.sum(grad_out_normed, axis=1, keepdims=True),
    )


def columns(*sums):
    lane = lax.broadcasted_iota(jnp.int32, (sums[0].shape[0], LANES), 1)
    high = [value.astype(BF16).astype(F32) for value in sums]
    out = jnp.zeros(lane.shape, F32)
    for n, value in enumerate(high + [value - top for value, top in zip(sums, high)]):
        out = jnp.where(lane == n, value, out)
    return out


def contract_back(grad_ref, other_ref, left_ref, right_ref, edges_ref, own, other, natural, edges):
    core, first = lax.axis_index("c"), first_half()
    own[...] = grad_ref[...].astype(F32)
    other[...] = other_ref[...].astype(F32)
    chips = own.shape[0] // 8
    for ch in range(2):
        halves = []
        for jh in range(2):
            halves.append(
                jnp.concatenate(
                    [rows[every(ch * 4 + 2 * r + jh, chips, 8), :] for rows in (own, other) for r in range(2)], axis=0
                )
            )
        grad = jnp.concatenate(halves, axis=1)
        grad_right = dot_nn(jnp.transpose(grad).astype(BF16), left_ref[ch])
        grad_left = dot_nn(grad.astype(BF16), right_ref[ch])
        natural[: 4 * chips, :] = grad_right[:, :LANES]
        natural[4 * chips :, :] = grad_right[:, LANES:]
        for c in range(2):
            for r in range(2):
                for kh in range(2):
                    at = slice(kh * LANES, (kh + 1) * LANES)
                    mine = grad_left[r * chips : (r + 1) * chips, at]
                    theirs = grad_left[(2 + r) * chips : (3 + r) * chips, at]
                    edges[every(ch * 8 + 4 * c + 2 * r + kh, chips, 16), :] = jnp.where(
                        first,
                        jnp.where(core == c, mine, theirs),
                        natural[every(kh * 4 * chips + 2 * c + r, chips, 4), :],
                    )
    edges_ref[...] = edges[...].astype(BF16)


def rear(
    edges_ref, factors_ref, normed_t_ref, hat_t_ref, w_in_ref, gate_term_ref, keep_ref, got_ref, vectors_ref,
    parts_ref, grad_normed_ref, give_ref, rows, parts,
):
    core, first = lax.axis_index("c"), first_half()
    hidden = w_in_ref.shape[1] // 4
    cells = gate_term_ref.shape[1]
    rows[...] = edges_ref[...].astype(F32)
    pieces = []
    for u in range(8):
        at = slice(u * LANES, (u + 1) * LANES)
        grad = rows[every(u, hidden, 8), :]
        pieces.append(
            jnp.concatenate([grad * factors_ref[:hidden, at], grad * factors_ref[hidden:, at]], axis=0).astype(BF16)
        )
    grad_projected = jnp.concatenate(pieces, axis=1)
    w_in_part = dot_nt(normed_t_ref[...], grad_projected)
    w_in = w_in_ref[...].astype(F32)
    w_in = jnp.where(first, w_in[:, : 2 * hidden], w_in[:, 2 * hidden :]).astype(BF16)
    grad_normed = dot_nn(w_in, grad_projected)
    low, high = grad_normed[:, :cells], grad_normed[:, cells:]
    gate_term = gate_term_ref[...]
    low = low + jnp.where(core == 0, gate_term, 0.0)
    high = high + jnp.where(core == 0, 0.0, gate_term)
    grad_normed_ref[...] = jnp.where(core == 0, low, high)
    give_ref[...] = jnp.where(core == 0, high, low)
    channels = w_in_part.shape[0]
    for t in range(2):
        parts[every(t, channels, 4), :] = w_in_part[:, t * LANES : (t + 1) * LANES]
    parts[every(2, channels, 4), :] = keep_ref[...] + got_ref[...]
    gain = jnp.sum(low * hat_t_ref[:, :cells] + high * hat_t_ref[:, cells:], axis=1, keepdims=True)
    parts[every(3, channels, 4), :] = columns(
        gain, jnp.sum(low + high, axis=1, keepdims=True), vectors_ref[:, :1], vectors_ref[:, 1:2]
    )
    parts_ref[...] = parts[...].astype(BF16)


def beside_rear(grad_normed_ref, got_ref, hat_t_ref, scale_ref, norms_ref, pair_grad_ref):
    hat = hat_t_ref[...]
    scaled = (grad_normed_ref[...] + got_ref[...]) * column(norms_ref[:1, :])
    grad = scale_ref[:1, :] * (
        scaled
        - jnp.mean(scaled, axis=0, keepdims=True)
        - hat * jnp.mean(scaled * hat, axis=0, keepdims=True)
    )
    pair_grad_ref[...] = jnp.transpose(grad).astype(BF16)


def split_vectors(sums, count):
    at = every(3, count, 4)
    values = sums[at, :]
    sums[at, :] = columns(*(values[:, n : n + 1] + values[:, n + 4 : n + 5] for n in range(4)))


def reduce_share(parts_ref, share_ref):
    share_ref[...] = jnp.sum(parts_ref[...].astype(F32).reshape(-1, 8, LANES), axis=0)


def spread(share_ref, got_ref, copies_ref, sums):
    sums[...] = share_ref[...] + got_ref[...]
    split_vectors(sums, 2)
    copies_ref[...] = (
        jnp.broadcast_to(sums[...][None], (copies_ref.shape[0] // 8, 8, LANES))
        .reshape(copies_ref.shape)
        .astype(BF16)
    )


def finish(
    own_ref, other_ref, w_in_ref, w_gate_ref, w_out_ref, in_gain_ref, in_bias_ref, out_gain_ref, out_bias_ref,
    low, high,
):
    first = first_half()
    own, other = own_ref[...].astype(F32), other_ref[...].astype(F32)
    low[...] = jnp.where(first, own, other)
    high[...] = jnp.where(first, other, own)
    channels = w_in_ref.shape[0]
    for t in range(2):
        w_in_ref[:, t * LANES : (t + 1) * LANES] = low[every(t, channels, 4), :]
        w_in_ref[:, (2 + t) * LANES : (3 + t) * LANES] = high[every(t, channels, 4), :]
    w_gate_ref[...] = low[every(2, channels, 4), :]
    w_out_ref[...] = high[every(2, channels, 4), :]
    sums = jnp.transpose(low[every(3, channels, 4), :] + high[every(3, channels, 4), :])
    sums = sums[:4] + sums[4:8]
    in_gain_ref[...], in_bias_ref[...] = sums[:1], sums[1:2]
    out_gain_ref[...], out_bias_ref[...] = sums[2:3], sums[3:4]


def on_device(
    pair, grad_out, w_in, w_gate, w_out, ln_in_gain, ln_in_bias, ln_out_gain, ln_out_bias
):
    shape = pair.shape
    channels = shape[3]
    hidden = w_out.shape[0]
    cells = shape[1] * shape[2]
    full_len = shape[2]
    pair2 = pair.reshape(cells, channels)
    grad2 = grad_out.reshape(cells, channels)
    in_gain_row, in_bias_row = ln_in_gain.reshape(1, -1), ln_in_bias.reshape(1, -1)
    out_gain_row, out_bias_row = ln_out_gain.reshape(1, -1), ln_out_bias.reshape(1, -1)
    grid = (hidden, cells)
    quarter = (4 * hidden, LANES)
    whole = (8 * hidden, LANES)
    to_chips = lambda a: lax.all_to_all(a, CHIPS, 0, 0, tiled=True)
    stay = lambda a: pltpu.with_memory_space_constraint(a, pltpu.HBM)
    swap = lambda a: lax.ppermute(a, "c", SWAP)

    edges, normed, w_in_t, norms = call(
        front, [(whole, BF16), ((cells, channels), BF16), ((4 * hidden, channels), BF16), ((8, LANES), F32)],
        [
            whole, pltpu.VMEM((cells, channels), BF16), pltpu.VMEM(w_in.shape, BF16), (1, channels), (1, channels),
            (1, channels), (1, channels),
            pltpu.SemaphoreType.DMA((6,)),
        ],
        far=6,
    )(stay(pair2), stay(in_gain_row), stay(in_bias_row), stay(w_in), stay(out_gain_row), stay(out_bias_row))
    own, normed, pair_again = lax.optimization_barrier((to_chips(edges), normed, pair2))
    other = swap(own)
    pair_other = swap(pair_again)
    normed_t, hat_t, scale, factors, grad_t, gate_t, grad_lin, grad_out_normed, scaled, mean = call(
        beside_front,
        [
            (grid, BF16), (grid, F32), ((8, cells), F32), ((2 * hidden, cells), F32), (grid, F32), (grid, F32),
            (grid, BF16), (grid, F32), (grid, F32), ((8, cells), F32),
        ],
        work=1 << 28,
    )(normed, pair2, grad2, w_in_t, w_gate, w_out, norms)
    other, normed_t, pair_other = lax.optimization_barrier((other, normed_t, pair_other))
    product, left, right = call(
        contract,
        [(quarter, BF16), ((2, full_len, full_len), BF16), ((2, full_len, full_len), BF16)],
        [whole, whole, quarter, quarter],
    )(own, other)
    product = to_chips(product)
    (grad_product,) = call(middle, [(quarter, BF16)], [quarter, quarter])(product, scaled, mean)
    grad_cols = to_chips(grad_product)
    grad_cols, product, pair_other = lax.optimization_barrier((grad_cols, product, pair_other))
    grad_other = swap(grad_cols)
    keep, give, vectors, gate_term = call(
        beside_middle,
        [((hidden, channels), F32), ((channels, channels), F32), ((hidden, LANES), F32), (grid, F32)],
        [quarter],
        work=1 << 28,
    )(product, grad_out_normed, grad_lin, grad_t, gate_t, normed_t, w_out, w_gate, norms)
    both = (channels, 2 * cells)
    both_normed, both_hat, both_factors = call(
        beside_back, [(both, BF16), (both, F32), ((2 * hidden, 2 * cells), F32)], work=1 << 28
    )(pair_other, norms, w_in_t, normed_t, hat_t, factors)
    grad_other, gate_term, both_hat = lax.optimization_barrier((grad_other, gate_term, both_hat))
    got = swap(give)
    (grad_edges,) = call(contract_back, [(whole, BF16)], [quarter, quarter, quarter, whole])(
        grad_cols, grad_other, left, right
    )
    grad_edges, got = lax.optimization_barrier((grad_edges, got))
    grad_edges = to_chips(grad_edges)
    parts, grad_normed, give = call(
        rear, [(quarter, BF16), (grid, F32), (grid, F32)], [whole, quarter]
    )(grad_edges, both_factors, both_normed, both_hat, w_in, gate_term, keep, got, vectors)
    (share,) = call(reduce_share, [((8, LANES), F32)])(to_chips(parts))
    got = lax.ppermute(share, ("X", "c"), [(0, 3), (1, 2), (2, 1), (3, 0)])
    (copies,) = call(spread, [(quarter, BF16)], [(8, LANES)])(share, got)
    copies, give = lax.optimization_barrier((copies, give))
    part = swap(give)
    mine = to_chips(copies)
    mine, part, grad_normed = lax.optimization_barrier((mine, part, grad_normed))
    theirs = swap(mine)
    (pair_grad,) = call(beside_rear, [((cells, channels), BF16)], work=1 << 28)(
        grad_normed, part, hat_t, scale, norms
    )
    theirs, pair_grad = lax.optimization_barrier((theirs, pair_grad))
    w_in_total, w_gate_total, w_out_total, *vectors = call(
        finish,
        [(w_in.shape, F32), (w_gate.shape, F32), (w_out.shape, F32)] + [((1, LANES), F32)] * 4,
        [quarter, quarter],
    )(mine, theirs)
    return (
        pair_grad.reshape(shape),
        w_in_total,
        w_gate_total,
        w_out_total,
        *(vector.reshape(-1) for vector in vectors),
    )


def solution(mesh):
    fine = Mesh(mesh.devices.reshape(2, 2, 8, 4, 2), ("X", "x", "z", "y", "c"))
    cells = P("X", ("x", "z", "y", "c"), None, None)
    in_specs = (cells, cells, P(), P(), P(), P(), P(), P(), P())
    out_specs = (cells, P(), P(), P(), P(), P(), P(), P())
    return jax.shard_map(
        on_device, mesh=fine, in_specs=in_specs, out_specs=out_specs, check_vma=False
    )
```

```python
import functools

import jax
import jax.numpy as jnp
from jax import lax
from jax.experimental import pallas as pl
from jax.experimental.pallas import tpu as pltpu
from jax.sharding import Mesh, PartitionSpec as P

EPSILON = 1e-05
CHIPS = ("x", "z", "y")
SWAP = [(0, 1), (1, 0)]
LANES = 128
F32 = jnp.float32
BF16 = jnp.bfloat16


def call(body, outs, scratch=(), work=0, far=0):
    def run(*operands):
        return pl.pallas_call(
            body,
            out_shape=[jax.ShapeDtypeStruct(shape, dtype) for shape, dtype in outs],
            in_specs=[pl.BlockSpec(memory_space=pltpu.HBM)] * far
            + [pl.BlockSpec(memory_space=pltpu.VMEM)] * (len(operands) - far),
            out_specs=[pl.BlockSpec(memory_space=pltpu.VMEM)] * len(outs),
            scratch_shapes=[pltpu.VMEM(s, F32) if isinstance(s, tuple) else s for s in scratch],
            compiler_params=pltpu.CompilerParams(vmem_limit_bytes=8 * 1024 * 1024),
            cost_estimate=pl.CostEstimate(
                flops=work, bytes_accessed=1 << 20, transcendentals=0
            ),
        )(*operands)

    return run


def dot_nt(a, b):
    return lax.dot_general(a, b, (((1,), (1,)), ((), ())), preferred_element_type=F32)


def dot_nn(a, b):
    return lax.dot_general(a, b, (((1,), (0,)), ((), ())), preferred_element_type=F32)


def sigmoid(x):
    return jax.nn.sigmoid(x)


def first_half():
    return lax.axis_index("c") == lax.axis_index("X")


def every(start, count, stride):
    return pl.ds(start, count, stride=stride)


def column(row):
    return jnp.transpose(jnp.broadcast_to(row, (LANES, row.shape[1])))[:, :1]


def front(
    pair_far, gain_far, bias_far, w_in_far, out_gain_far, out_bias_far, edges_ref, normed_ref, w_in_t_ref, norms_ref,
    rows, pair_ref, w_in_ref, gain_ref, bias_ref, out_gain_ref, out_bias_ref, arrived,
):
    copies = [
        pltpu.make_async_copy(source, target, arrived.at[n])
        for n, (source, target) in enumerate(
            [(pair_far, pair_ref), (gain_far, gain_ref), (bias_far, bias_ref), (w_in_far, w_in_ref),
             (out_gain_far, out_gain_ref), (out_bias_far, out_bias_ref)]
        )
    ]
    for copy in copies:
        copy.start()
    for copy in copies[:3]:
        copy.wait()
    values = pair_ref[...].astype(F32)
    center = values - jnp.mean(values, axis=1, keepdims=True)
    scale = lax.rsqrt(jnp.mean(center * center, axis=1, keepdims=True) + EPSILON)
    normed = (center * scale * gain_ref[...] + bias_ref[...]).astype(BF16)
    normed_ref[...] = normed
    for copy in copies[3:]:
        copy.wait()
    norms = [gain_ref[...], bias_ref[...], out_gain_ref[...], out_bias_ref[...]]
    norms_ref[...] = jnp.concatenate(norms + norms, axis=0)
    w_in_t = jnp.transpose(w_in_ref[...].astype(F32)).astype(BF16)
    w_in_t_ref[...] = w_in_t
    hidden = w_in_t.shape[0] // 4
    for side in range(2):
        proj = dot_nt(w_in_t[2 * side * hidden : (2 * side + 1) * hidden], normed)
        gate = dot_nt(w_in_t[(2 * side + 1) * hidden : (2 * side + 2) * hidden], normed)
        value = sigmoid(gate) * proj
        for u in range(4):
            rows[every(4 * side + u, hidden, 8), :] = value[:, u * LANES : (u + 1) * LANES]
    edges_ref[...] = rows[...].astype(BF16)


def beside_front(
    normed_ref, pair_ref, grad_ref, w_in_t_ref, w_gate_ref, w_out_ref, norms_ref,
    normed_t_ref, hat_t_ref, scale_ref, factors_ref, grad_t_ref, gate_t_ref, grad_lin_ref,
    grad_out_normed_ref, scaled_ref, mean_ref,
):
    hidden = w_out_ref.shape[0]
    normed = normed_ref[...]
    normed_t_ref[...] = jnp.transpose(normed.astype(F32)).astype(BF16)
    values = jnp.transpose(pair_ref[...].astype(F32))
    center = values - jnp.mean(values, axis=0, keepdims=True)
    scale = lax.rsqrt(jnp.mean(center * center, axis=0, keepdims=True) + EPSILON)
    hat_t_ref[...] = center * scale
    scale_ref[...] = jnp.broadcast_to(scale, scale_ref.shape)
    grad_t = jnp.transpose(grad_ref[...].astype(F32))
    grad_t_ref[...] = grad_t
    w_gate_t = jnp.transpose(w_gate_ref[...].astype(F32)).astype(BF16)
    gate = sigmoid(dot_nt(w_gate_t, normed))
    gate_t_ref[...] = gate
    grad_lin = (grad_t * gate).astype(BF16)
    grad_lin_ref[...] = grad_lin
    grad_out_normed = dot_nn(w_out_ref[...], grad_lin)
    grad_out_normed_ref[...] = grad_out_normed
    scaled = grad_out_normed * column(norms_ref[2:3, :])
    scaled_ref[...] = scaled
    mean_ref[...] = jnp.broadcast_to(jnp.mean(scaled, axis=0, keepdims=True), mean_ref.shape)
    factors_ref[...] = factors_of(w_in_t_ref, normed)


def factors_of(w_in_t_ref, normed):
    hidden = w_in_t_ref.shape[0] // 4
    at = pl.multiple_of(jnp.where(first_half(), 0, 2 * hidden), LANES)
    proj = dot_nt(w_in_t_ref[pl.ds(at, hidden), :], normed)
    sig = sigmoid(dot_nt(w_in_t_ref[pl.ds(at + hidden, hidden), :], normed))
    return jnp.concatenate([sig, proj * sig * (1.0 - sig)], axis=0)


def beside_back(
    pair_ref, norms_ref, w_in_t_ref, normed_t_ref, hat_t_ref, factors_ref,
    both_normed_ref, both_hat_ref, both_factors_ref,
):
    core = lax.axis_index("c")
    cells = pair_ref.shape[0]
    values = pair_ref[...].astype(F32)
    center = values - jnp.mean(values, axis=1, keepdims=True)
    hat = center * lax.rsqrt(jnp.mean(center * center, axis=1, keepdims=True) + EPSILON)
    normed = (hat * norms_ref[:1, :] + norms_ref[1:2, :]).astype(BF16)
    for both_ref, own, other in [
        (both_normed_ref, normed_t_ref[...].astype(F32), jnp.transpose(normed.astype(F32))),
        (both_hat_ref, hat_t_ref[...], jnp.transpose(hat)),
        (both_factors_ref, factors_ref[...], factors_of(w_in_t_ref, normed)),
    ]:
        both_ref[:, :cells] = jnp.where(core == 0, own, other).astype(both_ref.dtype)
        both_ref[:, cells:] = jnp.where(core == 0, other, own).astype(both_ref.dtype)


def contract(own_ref, other_ref, product_ref, left_ref, right_ref, own, other, natural, rows):
    core = lax.axis_index("c")
    own[...] = own_ref[...].astype(F32)
    other[...] = other_ref[...].astype(F32)
    chips = own.shape[0] // 16
    for ch in range(2):
        halves = []
        for kh in range(2):
            halves.append(
                jnp.concatenate([own[every(ch * 8 + 2 * r + kh, chips, 16), :] for r in range(2)], axis=0)
            )
            for r in range(2):
                at = every(ch * 8 + 4 + 2 * r + kh, chips, 16)
                mine, theirs = own[at, :], other[at, :]
                base = kh * 4 * chips + r
                natural[every(base, chips, 4), :] = jnp.where(core == 0, mine, theirs)
                natural[every(base + 2, chips, 4), :] = jnp.where(core == 0, theirs, mine)
        left = jnp.concatenate(halves, axis=1).astype(BF16)
        right = jnp.concatenate([natural[: 4 * chips, :], natural[4 * chips :, :]], axis=1).astype(BF16)
        left_ref[ch, : 2 * chips] = left
        theirs = [
            jnp.concatenate([other[every(ch * 8 + 2 * r + kh, chips, 16), :] for r in range(2)], axis=0)
            for kh in range(2)
        ]
        left_ref[ch, 2 * chips :] = jnp.concatenate(theirs, axis=1).astype(BF16)
        right_ref[ch] = right
        product = dot_nt(left, right)
        for r in range(2):
            for jh in range(2):
                rows[every(ch * 4 + 2 * r + jh, chips, 8), :] = product[
                    r * chips : (r + 1) * chips, jh * LANES : (jh + 1) * LANES
                ]
    product_ref[...] = rows[...].astype(BF16)


def out_norm(values):
    center = values - jnp.mean(values, axis=0, keepdims=True)
    scale = lax.rsqrt(jnp.mean(center * center, axis=0, keepdims=True) + EPSILON)
    return center * scale, scale


def middle(product_ref, scaled_ref, mean_ref, grad_ref, rows, grads):
    hidden = scaled_ref.shape[0]
    rows[...] = product_ref[...].astype(F32)
    for u in range(4):
        hat, scale = out_norm(rows[every(u, hidden, 4), :])
        at = slice(u * LANES, (u + 1) * LANES)
        scaled = scaled_ref[:, at]
        both = jnp.mean(scaled * hat, axis=0, keepdims=True)
        grads[every(u, hidden, 4), :] = scale * (scaled - mean_ref[:1, at] - hat * both)
    grad_ref[...] = grads[...].astype(BF16)


def beside_middle(
    product_ref, grad_out_normed_ref, grad_lin_ref, grad_t_ref, gate_t_ref, normed_t_ref,
    w_out_ref, w_gate_ref, norms_ref, keep_ref, give_ref, vectors_ref, gate_term_ref,
    rows,
):
    hidden = w_out_ref.shape[0]
    rows[...] = product_ref[...].astype(F32)
    hats, normed = [], []
    gain, bias = column(norms_ref[2:3, :]), column(norms_ref[3:4, :])
    for u in range(4):
        hat, _ = out_norm(rows[every(u, hidden, 4), :])
        hats.append(hat)
        normed.append((hat * gain + bias).astype(BF16))
    hat = jnp.concatenate(hats, axis=1)
    out_normed = jnp.concatenate(normed, axis=1)
    w_out_t = jnp.transpose(w_out_ref[...].astype(F32)).astype(BF16)
    outlin = dot_nn(w_out_t, out_normed)
    gate = gate_t_ref[...]
    grad_gate = (grad_t_ref[...] * outlin * gate * (1.0 - gate)).astype(BF16)
    first = first_half()
    w_out_part = dot_nt(out_normed, grad_lin_ref[...])
    w_gate_part = dot_nt(normed_t_ref[...], grad_gate)
    keep_ref[...] = jnp.where(first, w_gate_part, w_out_part)
    give_ref[...] = jnp.where(first, w_out_part, w_gate_part)
    gate_term_ref[...] = dot_nn(w_gate_ref[...], grad_gate)
    grad_out_normed = grad_out_normed_ref[...]
    lane = lax.broadcasted_iota(jnp.int32, vectors_ref.shape, 1)
    vectors_ref[...] = jnp.where(
        lane == 0,
        jnp.sum(grad_out_normed * hat, axis=1, keepdims=True),
        jnp.sum(grad_out_normed, axis=1, keepdims=True),
    )


def columns(*sums):
    lane = lax.broadcasted_iota(jnp.int32, (sums[0].shape[0], LANES), 1)
    high = [value.astype(BF16).astype(F32) for value in sums]
    out = jnp.zeros(lane.shape, F32)
    for n, value in enumerate(high + [value - top for value, top in zip(sums, high)]):
        out = jnp.where(lane == n, value, out)
    return out


def contract_back(grad_ref, other_ref, left_ref, right_ref, edges_ref, own, other, natural, edges):
    core, first = lax.axis_index("c"), first_half()
    own[...] = grad_ref[...].astype(F32)
    other[...] = other_ref[...].astype(F32)
    chips = own.shape[0] // 8
    for ch in range(2):
        halves = []
        for jh in range(2):
            halves.append(
                jnp.concatenate(
                    [rows[every(ch * 4 + 2 * r + jh, chips, 8), :] for rows in (own, other) for r in range(2)], axis=0
                )
            )
        grad = jnp.concatenate(halves, axis=1)
        places = [(c, r, kh) for c in range(2) for r in range(2) for kh in range(2)]

        @pl.when(first)
        def _():
            grad_left = dot_nn(grad.astype(BF16), right_ref[ch])
            for c, r, kh in places:
                at = slice(kh * LANES, (kh + 1) * LANES)
                mine = grad_left[r * chips : (r + 1) * chips, at]
                theirs = grad_left[(2 + r) * chips : (3 + r) * chips, at]
                edges[every(ch * 8 + 4 * c + 2 * r + kh, chips, 16), :] = jnp.where(core == c, mine, theirs)

        @pl.when(jnp.logical_not(first))
        def _():
            grad_right = dot_nn(jnp.transpose(grad).astype(BF16), left_ref[ch])
            natural[: 4 * chips, :] = grad_right[:, :LANES]
            natural[4 * chips :, :] = grad_right[:, LANES:]
            for c, r, kh in places:
                edges[every(ch * 8 + 4 * c + 2 * r + kh, chips, 16), :] = natural[
                    every(kh * 4 * chips + 2 * c + r, chips, 4), :
                ]

    edges_ref[...] = edges[...].astype(BF16)


def rear(
    edges_ref, factors_ref, normed_t_ref, hat_t_ref, w_in_ref, gate_term_ref, keep_ref, got_ref, vectors_ref,
    parts_ref, grad_normed_ref, give_ref, rows, parts,
):
    core, first = lax.axis_index("c"), first_half()
    hidden = w_in_ref.shape[1] // 4
    cells = gate_term_ref.shape[1]
    rows[...] = edges_ref[...].astype(F32)
    pieces = []
    for u in range(8):
        at = slice(u * LANES, (u + 1) * LANES)
        grad = rows[every(u, hidden, 8), :]
        pieces.append(
            jnp.concatenate([grad * factors_ref[:hidden, at], grad * factors_ref[hidden:, at]], axis=0).astype(BF16)
        )
    grad_projected = jnp.concatenate(pieces, axis=1)
    w_in_part = dot_nt(normed_t_ref[...], grad_projected)
    w_in = w_in_ref[...].astype(F32)
    w_in = jnp.where(first, w_in[:, : 2 * hidden], w_in[:, 2 * hidden :]).astype(BF16)
    grad_normed = dot_nn(w_in, grad_projected)
    low, high = grad_normed[:, :cells], grad_normed[:, cells:]
    gate_term = gate_term_ref[...]
    low = low + jnp.where(core == 0, gate_term, 0.0)
    high = high + jnp.where(core == 0, 0.0, gate_term)
    grad_normed_ref[...] = jnp.where(core == 0, low, high)
    give_ref[...] = jnp.where(core == 0, high, low)
    channels = w_in_part.shape[0]
    for t in range(2):
        parts[every(t, channels, 4), :] = w_in_part[:, t * LANES : (t + 1) * LANES]
    parts[every(2, channels, 4), :] = keep_ref[...] + got_ref[...]
    gain = jnp.sum(low * hat_t_ref[:, :cells] + high * hat_t_ref[:, cells:], axis=1, keepdims=True)
    parts[every(3, channels, 4), :] = columns(
        gain, jnp.sum(low + high, axis=1, keepdims=True), vectors_ref[:, :1], vectors_ref[:, 1:2]
    )
    parts_ref[...] = parts[...].astype(BF16)


def beside_rear(grad_normed_ref, got_ref, hat_t_ref, scale_ref, norms_ref, pair_grad_ref):
    hat = hat_t_ref[...]
    scaled = (grad_normed_ref[...] + got_ref[...]) * column(norms_ref[:1, :])
    grad = scale_ref[:1, :] * (
        scaled
        - jnp.mean(scaled, axis=0, keepdims=True)
        - hat * jnp.mean(scaled * hat, axis=0, keepdims=True)
    )
    pair_grad_ref[...] = jnp.transpose(grad).astype(BF16)


def split_vectors(sums, count):
    at = every(3, count, 4)
    values = sums[at, :]
    sums[at, :] = columns(*(values[:, n : n + 1] + values[:, n + 4 : n + 5] for n in range(4)))


def reduce_share(parts_ref, share_ref):
    share_ref[...] = jnp.sum(parts_ref[...].astype(F32).reshape(-1, 8, LANES), axis=0)


def spread(share_ref, got_ref, copies_ref, sums):
    sums[...] = share_ref[...] + got_ref[...]
    split_vectors(sums, 2)
    copies_ref[...] = (
        jnp.broadcast_to(sums[...][None], (copies_ref.shape[0] // 8, 8, LANES))
        .reshape(copies_ref.shape)
        .astype(BF16)
    )


def finish(
    own_ref, other_ref, w_in_ref, w_gate_ref, w_out_ref, in_gain_ref, in_bias_ref, out_gain_ref, out_bias_ref,
    low, high,
):
    first = first_half()
    own, other = own_ref[...].astype(F32), other_ref[...].astype(F32)
    low[...] = jnp.where(first, own, other)
    high[...] = jnp.where(first, other, own)
    channels = w_in_ref.shape[0]
    for t in range(2):
        w_in_ref[:, t * LANES : (t + 1) * LANES] = low[every(t, channels, 4), :]
        w_in_ref[:, (2 + t) * LANES : (3 + t) * LANES] = high[every(t, channels, 4), :]
    w_gate_ref[...] = low[every(2, channels, 4), :]
    w_out_ref[...] = high[every(2, channels, 4), :]
    sums = jnp.transpose(low[every(3, channels, 4), :] + high[every(3, channels, 4), :])
    sums = sums[:4] + sums[4:8]
    in_gain_ref[...], in_bias_ref[...] = sums[:1], sums[1:2]
    out_gain_ref[...], out_bias_ref[...] = sums[2:3], sums[3:4]


def on_device(
    pair, grad_out, w_in, w_gate, w_out, ln_in_gain, ln_in_bias, ln_out_gain, ln_out_bias
):
    shape = pair.shape
    channels = shape[3]
    hidden = w_out.shape[0]
    cells = shape[1] * shape[2]
    full_len = shape[2]
    pair2 = pair.reshape(cells, channels)
    grad2 = grad_out.reshape(cells, channels)
    in_gain_row, in_bias_row = ln_in_gain.reshape(1, -1), ln_in_bias.reshape(1, -1)
    out_gain_row, out_bias_row = ln_out_gain.reshape(1, -1), ln_out_bias.reshape(1, -1)
    grid = (hidden, cells)
    quarter = (4 * hidden, LANES)
    whole = (8 * hidden, LANES)
    to_chips = lambda a: lax.all_to_all(a, CHIPS, 0, 0, tiled=True)
    stay = lambda a: pltpu.with_memory_space_constraint(a, pltpu.HBM)
    swap = lambda a: lax.ppermute(a, "c", SWAP)

    edges, normed, w_in_t, norms = call(
        front, [(whole, BF16), ((cells, channels), BF16), ((4 * hidden, channels), BF16), ((8, LANES), F32)],
        [
            whole, pltpu.VMEM((cells, channels), BF16), pltpu.VMEM(w_in.shape, BF16), (1, channels), (1, channels),
            (1, channels), (1, channels),
            pltpu.SemaphoreType.DMA((6,)),
        ],
        far=6,
    )(stay(pair2), stay(in_gain_row), stay(in_bias_row), stay(w_in), stay(out_gain_row), stay(out_bias_row))
    own, normed, pair_again = lax.optimization_barrier((to_chips(edges), normed, pair2))
    other = swap(own)
    pair_other = swap(pair_again)
    normed_t, hat_t, scale, factors, grad_t, gate_t, grad_lin, grad_out_normed, scaled, mean = call(
        beside_front,
        [
            (grid, BF16), (grid, F32), ((8, cells), F32), ((2 * hidden, cells), F32), (grid, F32), (grid, F32),
            (grid, BF16), (grid, F32), (grid, F32), ((8, cells), F32),
        ],
        work=1 << 28,
    )(normed, pair2, grad2, w_in_t, w_gate, w_out, norms)
    other, normed_t, pair_other = lax.optimization_barrier((other, normed_t, pair_other))
    product, left, right = call(
        contract,
        [(quarter, BF16), ((2, full_len, full_len), BF16), ((2, full_len, full_len), BF16)],
        [whole, whole, quarter, quarter],
    )(own, other)
    product = to_chips(product)
    (grad_product,) = call(middle, [(quarter, BF16)], [quarter, quarter])(product, scaled, mean)
    grad_cols = to_chips(grad_product)
    grad_cols, product, pair_other = lax.optimization_barrier((grad_cols, product, pair_other))
    grad_other = swap(grad_cols)
    keep, give, vectors, gate_term = call(
        beside_middle,
        [((hidden, channels), F32), ((channels, channels), F32), ((hidden, LANES), F32), (grid, F32)],
        [quarter],
        work=1 << 28,
    )(product, grad_out_normed, grad_lin, grad_t, gate_t, normed_t, w_out, w_gate, norms)
    both = (channels, 2 * cells)
    both_normed, both_hat, both_factors = call(
        beside_back, [(both, BF16), (both, F32), ((2 * hidden, 2 * cells), F32)], work=1 << 28
    )(pair_other, norms, w_in_t, normed_t, hat_t, factors)
    grad_other, gate_term, both_hat = lax.optimization_barrier((grad_other, gate_term, both_hat))
    got = swap(give)
    (grad_edges,) = call(contract_back, [(whole, BF16)], [quarter, quarter, quarter, whole])(
        grad_cols, grad_other, left, right
    )
    grad_edges, got = lax.optimization_barrier((grad_edges, got))
    grad_edges = to_chips(grad_edges)
    parts, grad_normed, give = call(
        rear, [(quarter, BF16), (grid, F32), (grid, F32)], [whole, quarter]
    )(grad_edges, both_factors, both_normed, both_hat, w_in, gate_term, keep, got, vectors)
    (share,) = call(reduce_share, [((8, LANES), F32)])(to_chips(parts))
    share, give = lax.optimization_barrier((share, give))
    got = lax.ppermute(share, ("X", "c"), [(0, 3), (1, 2), (2, 1), (3, 0)])
    (pair_grad,) = call(beside_rear, [((cells, channels), BF16)], work=1 << 28)(
        grad_normed, swap(give), hat_t, scale, norms
    )
    got, pair_grad = lax.optimization_barrier((got, pair_grad))
    (copies,) = call(spread, [(quarter, BF16)], [(8, LANES)])(share, got)
    mine = to_chips(copies)
    w_in_total, w_gate_total, w_out_total, *vectors = call(
        finish,
        [(w_in.shape, F32), (w_gate.shape, F32), (w_out.shape, F32)] + [((1, LANES), F32)] * 4,
        [quarter, quarter],
    )(mine, swap(mine))
    return (
        pair_grad.reshape(shape),
        w_in_total,
        w_gate_total,
        w_out_total,
        *(vector.reshape(-1) for vector in vectors),
    )


def solution(mesh):
    fine = Mesh(mesh.devices.reshape(2, 2, 8, 4, 2), ("X", "x", "z", "y", "c"))
    cells = P("X", ("x", "z", "y", "c"), None, None)
    in_specs = (cells, cells, P(), P(), P(), P(), P(), P(), P())
    out_specs = (cells, P(), P(), P(), P(), P(), P(), P())
    return jax.shard_map(
        on_device, mesh=fine, in_specs=in_specs, out_specs=out_specs, check_vma=False
    )
```
